256 devices in a mesh: tm: 64 (over z, y, core), tensor: 4 (over x).
Axes of the slice: x: 4, y: 4, z: 8, core: 2. Of those that a mesh axis runs over, the one named last changes fastest.
Arguments:
- frames_in: bfloat16 [64, 1024, 768], P('tm'), may hold values from -16 to 16
- norm_gain: float32 [768], replicated, may hold values from 0.1 to 1.9
- w_qkv: bfloat16 [768, 3, 768], P(None, None, 'tensor'), may hold values from -0.21650635 to 0.21650635
- w_out: bfloat16 [768, 768], P('tensor'), may hold values from -0.21875 to 0.21875
- keep_runs: int32 [64, 16, 2], replicated, may hold values from 0 to 1023, as said below
- out_cotangent: bfloat16 [64, 1024, 768], P('tm'), may hold values from -16 to 16
Outputs:
- block_out: bfloat16 [64, 1024, 768], P('tm', None, 'tensor')
- grad_in: bfloat16 [64, 1024, 768], P('tm', None, 'tensor')
- grad_qkv: bfloat16 [768, 3, 768], P('tm', None, 'tensor')
- grad_proj: bfloat16 [768, 768], P('tensor', 'tm')
- grad_gain: float32 [768], P('tensor')
The draws below stay inside these ranges and needn't reach their ends.
Inputs may be any that keep to these rules, and one draw needn't show every extreme that they name: keep_runs[t, r] = (first, length) is the r-th run of kept positions of frame t; the 16 runs of a frame are disjoint, in rising order, and lie within the frame's 1024 positions.
All inputs are finite; a program needn't handle non-finite values.
Results may differ from the reference program's by a relative error of at most 0.034.
Values may be sent and summed in bfloat16 or wider, within the bound.
A program may use at most 128 MiB of HBM per device.

```python
import jax
import jax.numpy as jnp
from jax import lax

D = 768
H = 12
P_SIZE = 1024
F_DEV = 1
R = 16
F = 64


def draw_keep_runs(key, part):
    run_block = P_SIZE // R
    length_key, offset_key = jax.random.split(jax.random.fold_in(key, 7))
    lengths = jax.random.randint(length_key, (F, R), 1, 4 * run_block // 5 + 1)
    offsets = jax.random.randint(offset_key, (F, R), 0, run_block - lengths + 1)
    starts = jnp.arange(R, dtype=jnp.int32)[None, :] * run_block + offsets
    return jnp.stack([starts, lengths], axis=-1).astype(jnp.int32)


def draw_frames_in(key, part):
    keys = jax.random.split(jax.random.fold_in(key, 11), 2)
    groups = F // F_DEV
    block_width = D // groups
    drawn = jax.random.normal(keys[0], (F, P_SIZE, D), jnp.float32)
    chosen = jax.random.permutation(keys[1], groups)
    frame_block = chosen[jnp.arange(F) // F_DEV]
    feature_block = jnp.arange(D) // block_width
    boost = jnp.where(feature_block[None, :] == frame_block[:, None], 3.0, 1.0)
    tokens = drawn * boost[:, None, :]
    return jnp.clip(tokens, -16.0, 16.0).astype(jnp.bfloat16)


def draw_w_qkv(key, part):
    base_key = jax.random.fold_in(jax.random.fold_in(key, 23), 0)
    limit = 6.0 * D ** (-0.5)
    base = jax.random.normal(base_key, (D, 3, D), jnp.float32) * D ** (-0.5)
    return jnp.clip(base, -limit, limit).astype(jnp.bfloat16)


def strengthened(drawn, key, source, target, blocks, factor):
    def block_of(axis_at):
        return (jnp.arange(drawn.shape[axis_at]) // (drawn.shape[axis_at] // blocks)).reshape((-1,) + (1,) * (drawn.ndim - 1 - axis_at))

    one_side = jax.random.permutation(key, blocks)[block_of(target)]
    far = (block_of(target) + blocks // 2) % blocks
    return jnp.where((block_of(source) == one_side) | (block_of(source) == far), factor * drawn, drawn)


def block_levels(stream_key, shape, cuts, smallest, largest):
    loudness = 1.0
    for dim, parts in cuts:
        draws = jax.random.uniform(jax.random.fold_in(jax.random.fold_in(stream_key, 6), dim), (parts,), jnp.float32, smallest / len(cuts), largest / len(cuts))
        loudness = loudness * jnp.repeat(jnp.exp(draws), shape[dim] // parts).reshape((-1,) + (1,) * (len(shape) - 1 - dim))
    return loudness


def centred(key, dims, deviation, most, cuts=(), kind=jnp.bfloat16):
    gain = block_levels(key, dims, cuts, -0.22, 0.18) if cuts else 1.0
    drawn = jax.random.normal(key, dims, jnp.float32) * deviation * gain
    return jnp.minimum(jnp.maximum(drawn, -most), most).astype(kind)


def noise_with(key, extent, width, most, shards, heavy, kind=jnp.bfloat16):
    drawn = width * jax.random.normal(key, extent, jnp.float32)
    if shards:
        drawn = drawn * block_levels(key, extent, shards, -0.22, 0.18)
    return jnp.clip(strengthened(drawn, jax.random.fold_in(key, 3), *heavy), -most, most).astype(kind)


def setup_inputs(seed: int = 0) -> dict:
    splits = jax.random.split(jax.random.key(seed), 7)
    return {
        "frames_in": draw_frames_in(jax.random.fold_in(splits[6], 71), 0),
        "norm_gain": jnp.clip(1.0 + 0.18 * jax.random.normal(splits[1], (D,), jnp.float32), 0.1, 1.9),
        "w_qkv": draw_w_qkv(jax.random.fold_in(splits[6], 71), 0),
        "w_out": centred(splits[3], (D, D), D ** -0.5, 0.21875, ((0, 4),)),
        "keep_runs": draw_keep_runs(jax.random.fold_in(splits[6], 71), 0),
        "out_cotangent": noise_with(splits[5], (F, P_SIZE, D), 1.0, 16.0, ((0, 64),), (0, 2, 64, 4.0)),
    }


epsilon = 1e-05

def kept_table(keep_runs, first_place, place_count):
    places = first_place + jnp.arange(place_count, dtype=jnp.int32)
    starts = keep_runs[:, :, 0:1]
    lengths = keep_runs[:, :, 1:2]
    inside = (places[None, None, :] >= starts) & (places[None, None, :] < starts + lengths)
    return lax.optimization_barrier(jnp.sum(inside.astype(jnp.int32), axis=1)).astype(jnp.int32)

def normalize(frames_in):
    frames_float = frames_in.astype(jnp.float32)
    centre = lax.optimization_barrier(jnp.mean(frames_float, axis=-1, keepdims=True))
    shifted = frames_float - centre
    spread = lax.optimization_barrier(jnp.mean(shifted * shifted, axis=-1, keepdims=True))
    inverse_spread = lax.rsqrt(spread + epsilon)
    return (frames_float, shifted * inverse_spread, inverse_spread)

def attend(packed, kept_mask):
    frames, places, row_width = packed.shape
    head_width = D // H
    pieces = packed.reshape(frames, places, 3, row_width // (3 * head_width), head_width)
    scores = jnp.einsum('tphd,uphd->phtu', pieces[:, :, 0].astype(jnp.float32), pieces[:, :, 1].astype(jnp.float32))
    scores = scores * head_width ** (-0.5)
    allowed = jnp.transpose(kept_mask)[:, None, None, :] > 0
    scores = jnp.where(allowed, scores, -1000000000.0)
    row_max = lax.optimization_barrier(jnp.max(scores, axis=-1, keepdims=True))
    exponent = jnp.exp(scores - row_max)
    weights = (exponent / lax.optimization_barrier(jnp.sum(exponent, axis=-1, keepdims=True))).astype(jnp.bfloat16)
    mixed_rows = jnp.einsum('phtu,uphd->tphd', weights.astype(jnp.float32), pieces[:, :, 2].astype(jnp.float32))
    mixed_rows = jnp.where(kept_mask[:, :, None, None] > 0, mixed_rows, 0.0)
    return mixed_rows.astype(jnp.bfloat16).reshape(frames, places, row_width // 3)

def forward(frames_in, norm_gain, w_qkv, w_out, kept_mask):
    frames_float, standard, inverse_spread = normalize(frames_in)
    normed = (standard * norm_gain).astype(jnp.bfloat16)
    packed = jnp.dot(normed.reshape(F * P_SIZE, D), w_qkv.reshape(D, 3 * D), preferred_element_type=jnp.float32)
    packed = packed.astype(jnp.bfloat16).reshape(F, P_SIZE, 3 * D)
    mixed_rows = attend(packed, kept_mask)
    branch = jnp.dot(mixed_rows.reshape(F * P_SIZE, D), w_out, preferred_element_type=jnp.float32).reshape(F, P_SIZE, D)
    return (frames_float + branch).astype(jnp.bfloat16)

def reference(frames_in, norm_gain, w_qkv, w_out, keep_runs, out_cotangent):
    kept_mask = kept_table(keep_runs, 0, P_SIZE)

    def apply_block(first_arg, second_arg, third_arg, fourth_arg):
        return forward(first_arg, second_arg, third_arg, fourth_arg, kept_mask)
    block_out, pullback = jax.vjp(apply_block, frames_in, norm_gain, w_qkv, w_out)
    grad_in, grad_gain, grad_qkv, grad_proj = pullback(out_cotangent)
    return (block_out, grad_in, grad_qkv, grad_proj, grad_gain)
```

```python
import jax
import jax.numpy as jnp
from jax import lax
from jax.experimental import pallas as pl
from jax.experimental.pallas import tpu as pltpu
from jax.sharding import PartitionSpec as P

MESH = pl.DeviceIdType.MESH
BF = jnp.bfloat16
F32 = jnp.float32
D = 768
EPS = 1e-05


def dot(a, b):
    return lax.dot_general(a, b, (((1,), (0,)), ((), ())), preferred_element_type=F32)


def dot_nt(a, b):
    return lax.dot_general(a, b, (((1,), (1,)), ((), ())), preferred_element_type=F32)


def dot_tn(a, b):
    return lax.dot_general(a, b, (((0,), (0,)), ((), ())), preferred_element_type=F32)


def iota(shape, axis):
    return lax.broadcasted_iota(jnp.int32, shape, axis)


def row_transpose_matrix():
    row = iota((256, 256), 0)
    col = iota((256, 256), 1)
    source = (row & 15) * 16 + (row >> 4)
    return jnp.where(col == source, 1.0, 0.0).astype(BF)


def feature_order_matrix():
    row = iota((D, 1), 0)
    core = (row >= 384).astype(jnp.int32)
    rest = row - 384 * core
    y = sum((rest >= 96 * k).astype(jnp.int32) for k in range(1, 4))
    rest = rest - 96 * y
    z = sum((rest >= 12 * k).astype(jnp.int32) for k in range(1, 8))
    rest = rest - 12 * z
    source = 12 * (z * 8 + y * 2 + core) + rest
    return jnp.where(iota((D, D), 1) == source, 1.0, 0.0).astype(BF)


def spread_matrix():
    row = iota((128, 96), 0)
    col = iota((128, 96), 1)
    inner = row & 15
    return jnp.where((inner < 12) & (col == (row >> 4) * 12 + inner), 1.0, 0.0).astype(BF)


def kernel(
    fr, ct, gain, w, runs,
    o_bo, o_gi, o_g, o_gg,
    r1, s2, r2, wb, std, nt, ctt, ncot, br, kept, pcm, gb, gc, hb, gx, hy, gy, gzs, gz,
    rb, t1, t2, ot, vg, vgc, vgx, vgy, vgz,
    a_s, a_r, b_s, b_r, w_s, w_r, f_s, f_r, c_s, c_r, x_s, x_r, y_s, y_r, z_s, z_r,
    p_s, p_r, q_s, q_r, vc_s, vc_r, vx_s, vx_r, vy_s, vy_r, vz_s, vz_r, l_s,
):
    m = lax.axis_index("tm")
    x = lax.axis_index("tensor")
    z = m // 8
    y = lax.rem(m // 2, 4)
    c = lax.rem(m, 2)
    me_zc = z * 2 + c

    def zc_peer(k):
        s = lax.rem(me_zc + k, 16)
        return s, ((s // 2) * 8 + y * 2 + lax.rem(s, 2), x)

    def yx_peer(k):
        q = lax.rem(x * 4 + y + k, 16)
        yy, xx = lax.rem(q, 4), q // 4
        return yy, xx, (z * 8 + yy * 2 + c, xx)

    def x_peer(k):
        xx = lax.rem(x + k, 4)
        return xx, (m, xx)

    def y_peer(k):
        yy = lax.rem(y + k, 4)
        return yy, (z * 8 + yy * 2 + c, x)

    def z_peer(k):
        zz = lax.rem(z + k, 8)
        return zz, (zz * 8 + y * 2 + c, x)

    core_peer = (z * 8 + y * 2 + (1 - c), x)

    def remote(src, dst, ss, rs, dev):
        return pltpu.make_async_remote_copy(
            src_ref=src, dst_ref=dst, send_sem=ss, recv_sem=rs, device_id=dev, device_id_type=MESH
        )

    def each(first, last, body):
        def step(k, carry):
            body(k)
            return carry
        lax.fori_loop(first, last, step, 0)

    barrier = pltpu.get_barrier_semaphore()

    def greet_zc(k):
        pl.semaphore_signal(barrier, inc=1, device_id=zc_peer(k)[1], device_id_type=MESH)

    def greet_yx(k):
        pl.semaphore_signal(barrier, inc=1, device_id=yx_peer(k)[2], device_id_type=MESH)

    each(1, 16, greet_zc)
    each(1, 16, greet_yx)

    own_w = pltpu.make_async_copy(w, wb.at[x], l_s.at[0])
    own_w.start()

    def own_rows(k):
        ref = (fr, ct)[k]
        return pltpu.make_async_copy(
            ref.at[pl.ds((me_zc * 4 + x) * 16, 16)], r1.at[k, me_zc], l_s.at[1 + k]
        )

    own_rows(0).start()
    own_rows(1).start()
    pl.semaphore_wait(barrier, 30)

    def token_copy(k, n):
        s, dev = zc_peer(n)
        rows = pl.ds((s * 4 + x) * 16, 16)
        return remote((fr, ct)[k].at[rows], r1.at[k, me_zc], a_s.at[k, s], a_r.at[k, me_zc], dev)

    def send_tokens(n):
        token_copy(0, n).start()
        token_copy(1, n).start()

    each(1, 16, send_tokens)

    half = pl.ds(c * 384, 384)

    def weight_copy(n):
        xx, dev = x_peer(n)
        return remote(w.at[half], wb.at[x, half], w_s.at[xx], w_r.at[x], dev)

    for n in (1, 3, 2):
        weight_copy(n).start()

    turn = row_transpose_matrix()
    order = feature_order_matrix()
    spread = spread_matrix()

    begin, end = runs[0], runs[1]
    for i in range(4):
        place = (me_zc * 4 + x) * 16 + y * 4 + i
        inside = jnp.where((begin <= place) & (place < end), 1.0, 0.0)
        kept[pl.ds(64 * i, 64), :] = jnp.broadcast_to(jnp.sum(inside, axis=1, keepdims=True), (64, 128))

    def got_tokens(n):
        s = lax.rem(me_zc + n, 16)
        for k in range(2):
            remote(fr.at[pl.ds(0, 16)], r1.at[k, s], a_s.at[k, s], a_r.at[k, s], core_peer).wait_recv()

    each(1, 16, got_tokens)
    own_rows(0).wait()
    own_rows(1).wait()
    for k in range(2):
        turned = dot(turn, r1[k].reshape(256, D)).astype(BF).reshape(4, 4, 16, D)
        s2[k] = turned

    def group_copy(n):
        yy, dev = y_peer(n)
        return remote(s2.at[:, yy], r2.at[:, :, y], b_s.at[yy], b_r.at[y], dev)

    for n in (1, 3, 2):
        group_copy(n).start()
    own_group = pltpu.make_async_copy(s2.at[:, y], r2.at[:, :, y], l_s.at[3])
    own_group.start()

    def forward_copy(n):
        xx = lax.rem(x + n, 4)
        return remote(wb.at[xx, half], wb.at[xx, half], f_s.at[xx], f_r.at[xx], core_peer)

    other_half = pl.ds((1 - c) * 384, 384)

    for n in (1, 3, 2):
        xx = lax.rem(x + n, 4)
        remote(w.at[half], wb.at[xx, half], w_s.at[xx], w_r.at[xx], core_peer).wait_recv()
        forward_copy(n).start()
    own_w.wait()

    for n in (1, 3, 2):
        yy = lax.rem(y + n, 4)
        remote(s2.at[:, yy], r2.at[:, :, yy], b_s.at[yy], b_r.at[yy], core_peer).wait_recv()
    own_group.wait()

    tokens = r2[0].reshape(256, D).astype(F32)
    centre = jnp.mean(tokens, axis=-1, keepdims=True)
    shifted = tokens - centre
    inverse = lax.rsqrt(jnp.mean(shifted * shifted, axis=-1, keepdims=True) + EPS)
    standard = shifted * inverse
    std[...] = standard
    normed = (standard * gain[...]).astype(BF)
    pcm[1] = normed
    nt[...] = dot_nt(order, normed).astype(BF)
    ctt[...] = dot_nt(order, r2[1].reshape(256, D)).astype(BF)
    ncot[...] = jnp.zeros((256, D), F32)
    br[...] = jnp.zeros((256, D), F32)

    lane = iota((64, 192), 1)
    head_mask = [(lane >= 64 * h) & (lane < 64 * h + 64) for h in range(3)]

    def stack_heads(rows):
        return jnp.concatenate([jnp.where(hm, rows, jnp.zeros_like(rows)) for hm in head_mask], axis=0)

    def pick_heads(rows):
        return jnp.where(head_mask[0], rows[0:64], jnp.where(head_mask[1], rows[64:128], rows[128:192]))

    def finish_core(jj):
        remote(gb.at[jj, c], gc.at[jj], c_s.at[jj], c_r.at[jj], core_peer).wait_recv()
        hb[jj] = (gb[jj, c].astype(F32) + gc[jj].astype(F32)).astype(BF)

    def share_copy(jj):
        xx, dev = x_peer(jj + 1)
        return remote(hb.at[jj], gx.at[x], x_s.at[xx], x_r.at[x], dev)

    def core_copy(jj):
        return remote(gb.at[jj, 1 - c], gc.at[jj], c_s.at[jj], c_r.at[jj], core_peer)

    def heads_step(jj, carry):
        j = lax.rem(x + jj + 1, 4)

        @pl.when(jj < 3)
        def _():
            remote(wb.at[j, other_half], wb.at[j, other_half], f_s.at[j], f_r.at[j], core_peer).wait_recv()

        packed = dot(pcm[1], wb[j]).astype(BF)
        cot = dot(r2[1].reshape(256, D), wb[j, :, 512:768]).astype(BF)[:, 64:256]
        for i in range(4):
            rows = slice(64 * i, 64 * i + 64)
            keep = kept[rows, 0:1] > 0
            keep3 = jnp.concatenate([kept[rows, 0:1]] * 3, axis=0) > 0
            q = packed[rows, 0:192]
            kk = packed[rows, 192:384]
            v = packed[rows, 384:576]
            mc = jnp.where(keep, cot[rows], jnp.zeros((64, 192), BF))
            kbd = stack_heads(kk)
            vbd = stack_heads(v)
            scores = jnp.where(keep3, dot_nt(kbd, q) * 0.125, -1000000000.0).reshape(3, 64, 64)
            top = jnp.max(scores, axis=1, keepdims=True)
            expo = jnp.exp(scores - top)
            weight = expo / jnp.sum(expo, axis=1, keepdims=True)
            wbf = weight.astype(BF).reshape(192, 64)
            mixed = jnp.where(keep, dot_tn(wbf, vbd), 0.0).astype(BF)
            dweight = dot_nt(vbd, mc).reshape(3, 64, 64)
            inner = jnp.sum(dweight * weight, axis=1, keepdims=True)
            dscore = (weight * (dweight - inner) * 0.125).astype(BF).reshape(192, 64)
            dq = dot_tn(dscore, kbd).astype(BF)
            dk = pick_heads(dot(dscore, q)).astype(BF)
            dv = pick_heads(dot(wbf, mc)).astype(BF)
            pcm[0, rows, 0:192] = dq
            pcm[0, rows, 192:384] = dk
            pcm[0, rows, 384:576] = dv
            pcm[0, rows, 576:768] = mixed
        low = iota((256, 256), 1) < 64
        tail = pcm[0, :, 512:768]
        tail_qkv = jnp.where(low, tail, jnp.zeros_like(tail))
        tail_mix = jnp.where(low, jnp.zeros_like(tail), tail)
        for h in range(2):
            rows = slice(384 * h, 384 * h + 384)
            gb[jj, h, :, 0:512] = dot(nt[rows, :], pcm[0, :, 0:512]).astype(BF)
            gb[jj, h, :, 512:768] = (dot(nt[rows, :], tail_qkv) + dot(ctt[rows, :], tail_mix)).astype(BF)
        core_copy(jj).start()
        wj_tail = wb[j, :, 512:768]
        ncot[...] += dot_nt(pcm[0, :, 0:512], wb[j, :, 0:512]) + dot_nt(tail_qkv, wj_tail)
        br[...] += dot_nt(tail_mix, wj_tail)

        @pl.when(jj > 0)
        def _():
            finish_core(jj - 1)
            share_copy(jj - 1).start()

        return carry

    lax.fori_loop(0, 4, heads_step, 0)

    block = (r2[0].reshape(256, D).astype(F32) + br[...]).astype(BF)
    cotangent = ncot[...].astype(BF).astype(F32)
    standard = std[...]
    scaled = cotangent * gain[...]
    mean_plain = jnp.mean(scaled, axis=-1, keepdims=True)
    mean_cross = jnp.mean(scaled * standard, axis=-1, keepdims=True)
    tokens = r2[0].reshape(256, D).astype(F32)
    centre = jnp.mean(tokens, axis=-1, keepdims=True)
    shifted = tokens - centre
    inverse = lax.rsqrt(jnp.mean(shifted * shifted, axis=-1, keepdims=True) + EPS)
    through = inverse * (scaled - mean_plain - standard * mean_cross)
    grad_in = (r2[1].reshape(256, D).astype(F32) + through).astype(BF)
    for xx in range(4):
        cols = slice(192 * xx, 192 * xx + 192)
        rb[xx] = jnp.concatenate([block[:, cols], grad_in[:, cols]], axis=1).reshape(4, 4, 16, 384)

    def result_copy(n):
        yy, xx, dev = yx_peer(n)
        return remote(rb.at[xx, :, yy], t1.at[x, y], p_s.at[xx, yy], p_r.at[x, y], dev)

    def send_result(n):
        result_copy(n).start()

    each(1, 16, send_result)
    own_result = pltpu.make_async_copy(rb.at[x, :, y], t1.at[x, y], l_s.at[4])
    own_result.start()

    gain_part = jnp.sum(cotangent * standard, axis=0, keepdims=True)
    vg[0] = jnp.concatenate(
        [gain_part[:, 192 * k : 192 * k + 192] for k in range(4)] + [jnp.zeros((4, 192), F32)], axis=0
    )
    gain_core = remote(vg.at[0], vgc, vc_s, vc_r, core_peer)
    gain_core.start()
    finish_core(3)
    gain_core.wait_recv()
    vg[1] = vg[0] + vgc[...]

    def gain_x(n):
        xx, dev = x_peer(n)
        return remote(vg.at[1], vgx.at[x], vx_s.at[xx], vx_r.at[x], dev)

    for n in range(1, 4):
        gain_x(n).start()

    own_result.wait()

    def place_copy(xx, n):
        s, dev = zc_peer(n)
        return remote(
            t2.at[xx, s], ot.at[me_zc, xx], q_s.at[xx, s], q_r.at[xx, me_zc], dev
        )

    def own_place(xx):
        return pltpu.make_async_copy(t2.at[xx, me_zc], ot.at[me_zc, xx], l_s.at[5 + xx])

    def group_step(n, carry):
        xx = lax.rem(x + n, 4)

        def got(k):
            yy = lax.rem(y + k, 4)

            @pl.when((n > 0) | (k > 0))
            def _():
                remote(rb.at[xx, :, yy], t1.at[xx, yy], p_s.at[xx, yy], p_r.at[xx, yy], core_peer).wait_recv()

        each(0, 4, got)
        t2[xx] = dot(turn, t1[xx].reshape(256, 384)).astype(BF).reshape(16, 16, 384)
        each(1, 16, lambda k: place_copy(xx, k).start())
        own_place(xx).start()
        return carry

    lax.fori_loop(0, 4, group_step, 0)

    total = hb[3].astype(F32)
    for n in range(1, 4):
        xx = lax.rem(x + n, 4)
        remote(hb.at[0], gx.at[xx], x_s.at[xx], x_r.at[xx], core_peer).wait_recv()
        total = total + gx[xx].astype(F32)
    hy[...] = total.astype(BF).reshape(4, 96, D)
    gain_total = vg[1]
    for n in range(1, 4):
        xx = lax.rem(x + n, 4)
        remote(vg.at[1], vgx.at[xx], vx_s.at[xx], vx_r.at[xx], core_peer).wait_recv()
        gain_total = gain_total + vgx[xx]
    vg[2] = gain_total

    def grad_y(n):
        yy, dev = y_peer(n)
        return remote(hy.at[yy], gy.at[y], y_s.at[yy], y_r.at[y], dev)

    def gain_y(n):
        yy, dev = y_peer(n)
        return remote(vg.at[2], vgy.at[y], vy_s.at[yy], vy_r.at[y], dev)

    for n in range(1, 4):
        grad_y(n).start()
        gain_y(n).start()
    total = hy[y].astype(F32)
    gain_total = vg[2]
    for n in range(1, 4):
        yy = lax.rem(y + n, 4)
        remote(hy.at[yy], gy.at[yy], y_s.at[yy], y_r.at[yy], core_peer).wait_recv()
        remote(vg.at[2], vgy.at[yy], vy_s.at[yy], vy_r.at[yy], core_peer).wait_recv()
        total = total + gy[yy].astype(F32)
        gain_total = gain_total + vgy[yy]
    gzs[...] = dot(spread, total.astype(BF)).astype(BF).reshape(8, 16, D)
    vg[3] = gain_total

    def grad_z(n):
        zz, dev = z_peer(n)
        return remote(gzs.at[zz], gz.at[z], z_s.at[zz], z_r.at[z], dev)

    def gain_z(n):
        zz, dev = z_peer(n)
        return remote(vg.at[3], vgz.at[z], vz_s.at[zz], vz_r.at[z], dev)

    for n in range(1, 8):
        grad_z(n).start()
        gain_z(n).start()
    total = gzs[z].astype(F32)
    gain_total = vg[3]
    for n in range(1, 8):
        zz = lax.rem(z + n, 8)
        remote(gzs.at[zz], gz.at[zz], z_s.at[zz], z_r.at[zz], core_peer).wait_recv()
        remote(vg.at[3], vgz.at[zz], vz_s.at[zz], vz_r.at[zz], core_peer).wait_recv()
        total = total + gz[zz].astype(F32)
        gain_total = gain_total + vgz[zz]
    o_g[...] = total.astype(BF)
    o_gg[...] = jnp.sum(jnp.where(iota((8, 192), 0) == x, gain_total, 0.0), axis=0, keepdims=True)

    def placed(xx):
        own_place(xx).wait()

        def one(k):
            s = lax.rem(me_zc + k, 16)
            remote(t2.at[xx, s], ot.at[s, xx], q_s.at[xx, s], q_r.at[xx, s], core_peer).wait_recv()

        each(1, 16, one)

    each(0, 4, placed)
    results = ot[...].reshape(1024, 384)
    o_bo[...] = results[:, 0:192]
    o_gi[...] = results[:, 192:384]

    def sent_zc(n):
        token_copy(0, n).wait_send()
        token_copy(1, n).wait_send()
        result_copy(n).wait_send()
        each(0, 4, lambda xx: place_copy(xx, n).wait_send())

    each(1, 16, sent_zc)
    for n in range(1, 4):
        weight_copy(n).wait_send()
        forward_copy(n).wait_send()
        group_copy(n).wait_send()
        gain_x(n).wait_send()
        grad_y(n).wait_send()
        gain_y(n).wait_send()
    each(0, 4, lambda jj: core_copy(jj).wait_send())
    each(0, 3, lambda jj: share_copy(jj).wait_send())
    for n in range(1, 8):
        grad_z(n).wait_send()
        gain_z(n).wait_send()
    gain_core.wait_send()


def body(frames_in, norm_gain, w_qkv, w_out, keep_runs, out_cotangent):
    w_all = jnp.concatenate([w_qkv.reshape(D, 576), w_out.T], axis=1)
    runs = keep_runs.reshape(8, 4, 2, 16, 2).transpose(4, 1, 0, 2, 3).reshape(2, 64, 16)
    runs = jnp.stack([runs[0], runs[0] + runs[1]])
    v = lambda shape, dt=BF: pltpu.VMEM(shape, dt)
    dma = pltpu.SemaphoreType.DMA
    any_spec = pl.BlockSpec(memory_space=pl.ANY)
    vmem_spec = pl.BlockSpec(memory_space=pltpu.VMEM)
    block_out, grad_in, grads, grad_gain = pl.pallas_call(
        kernel,
        out_shape=(
            jax.ShapeDtypeStruct((1024, 192), BF),
            jax.ShapeDtypeStruct((1024, 192), BF),
            jax.ShapeDtypeStruct((16, D), BF),
            jax.ShapeDtypeStruct((1, 192), F32),
        ),
        in_specs=[any_spec, any_spec, vmem_spec, any_spec, vmem_spec],
        out_specs=(vmem_spec,) * 4,
        scratch_shapes=[
            v((2, 16, 16, D)),
            v((2, 4, 4, 16, D)),
            v((2, 4, 4, 16, D)),
            v((4, D, D)),
            v((256, D), F32),
            v((D, 256)),
            v((D, 256)),
            v((256, D), F32),
            v((256, D), F32),
            v((256, 128), F32),
            v((2, 256, D)),
            v((4, 2, 384, D)),
            v((4, 384, D)),
            v((4, 384, D)),
            v((4, 384, D)),
            v((4, 96, D)),
            v((4, 96, D)),
            v((8, 16, D)),
            v((8, 16, D)),
            v((4, 4, 4, 16, 384)),
            v((4, 4, 4, 16, 384)),
            v((4, 16, 16, 384)),
            v((16, 4, 16, 384)),
            v((4, 8, 192), F32),
            v((8, 192), F32),
            v((4, 8, 192), F32),
            v((4, 8, 192), F32),
            v((8, 8, 192), F32),
            dma((2, 16)), dma((2, 16)),
            dma((4,)), dma((4,)),
            dma((4,)), dma((4,)),
            dma((4,)), dma((4,)),
            dma((4,)), dma((4,)),
            dma((4,)), dma((4,)),
            dma((4,)), dma((4,)),
            dma((8,)), dma((8,)),
            dma((4, 4)), dma((4, 4)),
            dma((4, 16)), dma((4, 16)),
            dma(()), dma(()),
            dma((4,)), dma((4,)),
            dma((4,)), dma((4,)),
            dma((8,)), dma((8,)),
            dma((9,)),
        ],
        compiler_params=pltpu.CompilerParams(
            collective_id=0, has_side_effects=True, vmem_limit_bytes=56 << 20
        ),
        cost_estimate=pl.CostEstimate(flops=5 * 10**9, bytes_accessed=10**7, transcendentals=200000),
        name="block",
    )(
        frames_in.reshape(1024, D), out_cotangent.reshape(1024, D), norm_gain.reshape(1, D), w_all, runs
    )
    return (
        block_out.reshape(1, 1024, 192),
        grad_in.reshape(1, 1024, 192),
        grads[:12, :576].reshape(12, 3, 192),
        grads[:12, 576:].T,
        grad_gain.reshape(192),
    )


def solution(mesh):
    in_specs = (
        P("tm", None, None),
        P(),
        P(None, None, "tensor"),
        P("tensor", None),
        P(),
        P("tm", None, None),
    )
    out_specs = (
        P("tm", None, "tensor"),
        P("tm", None, "tensor"),
        P("tm", None, "tensor"),
        P("tensor", "tm"),
        P("tensor"),
    )
    return jax.shard_map(body, mesh=mesh, in_specs=in_specs, out_specs=out_specs, check_vma=False)
```

```python
import jax
import jax.numpy as jnp
from jax import lax
from jax.experimental import pallas as pl
from jax.experimental.pallas import tpu as pltpu
from jax.sharding import PartitionSpec as P

MESH = pl.DeviceIdType.MESH
BF = jnp.bfloat16
F32 = jnp.float32
D = 768
EPS = 1e-05


def dot(a, b):
    return lax.dot_general(a, b, (((1,), (0,)), ((), ())), preferred_element_type=F32)


def dot_nt(a, b):
    return lax.dot_general(a, b, (((1,), (1,)), ((), ())), preferred_element_type=F32)


def dot_tn(a, b):
    return lax.dot_general(a, b, (((0,), (0,)), ((), ())), preferred_element_type=F32)


def iota(shape, axis):
    return lax.broadcasted_iota(jnp.int32, shape, axis)


def row_transpose_matrix():
    row = iota((256, 256), 0)
    col = iota((256, 256), 1)
    source = (row & 15) * 16 + (row >> 4)
    return jnp.where(col == source, 1.0, 0.0).astype(BF)


def feature_order_matrix():
    row = iota((D, 1), 0)
    core = (row >= 384).astype(jnp.int32)
    rest = row - 384 * core
    y = sum((rest >= 96 * k).astype(jnp.int32) for k in range(1, 4))
    rest = rest - 96 * y
    z = sum((rest >= 12 * k).astype(jnp.int32) for k in range(1, 8))
    rest = rest - 12 * z
    source = 12 * (z * 8 + y * 2 + core) + rest
    return jnp.where(iota((D, D), 1) == source, 1.0, 0.0).astype(BF)


def spread_matrix():
    row = iota((128, 96), 0)
    col = iota((128, 96), 1)
    inner = row & 15
    return jnp.where((inner < 12) & (col == (row >> 4) * 12 + inner), 1.0, 0.0).astype(BF)


def frame_order_matrix():
    row = iota((64, 64), 0)
    source = ((row >> 1) & 7) * 8 + (row >> 4) * 2 + (row & 1)
    return jnp.where(iota((64, 64), 1) == source, 1.0, 0.0).astype(BF)


def unpair_matrix():
    row = iota((256, 256), 0)
    col = iota((256, 256), 1)
    return jnp.where(col == (row & 127) * 2 + (row >> 7), 1.0, 0.0).astype(BF)


def kernel(
    fr, ct, gain, wq, wo, runs,
    o_bo, o_gi, o_gq, o_gp, o_gg,
    r1, s2, r2, wb, std, inv, nrm, nt, ctt, ncot, br, kept, keptw, qkv, wts, mx, pcm,
    gb, gc, hb, gx, gy1, hy1, gx2, hx, gy2, gzs, gz,
    rb, t1, t2, ot, vg, vgc, vgx, vgy, vgz,
    a_s, a_r, b_s, b_r, w_s, w_r, f_s, f_r, c_s, c_r, x_s, x_r, y1_s, y1_r, x2_s, x2_r,
    y2_s, y2_r, z_s, z_r, p_s, p_r, q_s, q_r, vc_s, vc_r, vx_s, vx_r, vy_s, vy_r, vz_s, vz_r, l_s,
):
    m = lax.axis_index("tm")
    x = lax.axis_index("tensor")
    z = m // 8
    y = lax.rem(m // 2, 4)
    c = lax.rem(m, 2)
    me_zc = z * 2 + c

    def zc_peer(k):
        s = lax.rem(me_zc + k, 16)
        return s, ((s // 2) * 8 + y * 2 + lax.rem(s, 2), x)

    def yx_peer(k):
        q = lax.rem(x * 4 + y + k, 16)
        yy, xx = lax.rem(q, 4), q // 4
        return yy, xx, (z * 8 + yy * 2 + c, xx)

    def x_peer(k):
        xx = lax.rem(x + k, 4)
        return xx, (m, xx)

    def y_peer(k):
        yy = lax.rem(y + k, 4)
        return yy, (z * 8 + yy * 2 + c, x)

    def z_peer(k):
        zz = lax.rem(z + k, 8)
        return zz, (zz * 8 + y * 2 + c, x)

    core_peer = (z * 8 + y * 2 + (1 - c), x)
    x_right, x_left, x_far = lax.rem(x + 1, 4), lax.rem(x + 3, 4), lax.rem(x + 2, 4)

    def remote(src, dst, ss, rs, dev):
        return pltpu.make_async_remote_copy(
            src_ref=src, dst_ref=dst, send_sem=ss, recv_sem=rs, device_id=dev, device_id_type=MESH
        )

    def arrive(dst, rs):
        remote(dst, dst, l_s.at[9], rs, core_peer).wait_recv()

    def each(first, last, body):
        def step(k, carry):
            body(k)
            return carry
        lax.fori_loop(first, last, step, 0)

    barrier = pltpu.get_barrier_semaphore()

    def greet(k):
        pl.semaphore_signal(barrier, inc=1, device_id=zc_peer(k)[1], device_id_type=MESH)
        pl.semaphore_signal(barrier, inc=1, device_id=yx_peer(k)[2], device_id_type=MESH)

    each(1, 16, greet)

    own_w = [
        pltpu.make_async_copy(wq, wb.at[x, pl.ds(0, 576)], l_s.at[0]),
        pltpu.make_async_copy(wo, wb.at[x, pl.ds(576, 192)], l_s.at[3]),
    ]
    for copy in own_w:
        copy.start()

    def own_rows(k):
        ref = (fr, ct)[k]
        return pltpu.make_async_copy(
            ref.at[pl.ds((me_zc * 4 + x) * 16, 16)], r1.at[k, me_zc], l_s.at[1 + k]
        )

    own_rows(0).start()
    own_rows(1).start()
    turn = row_transpose_matrix()
    pl.semaphore_wait(barrier, 30)

    def token_copy(k, n):
        s, dev = zc_peer(n)
        rows = pl.ds((s * 4 + x) * 16, 16)
        return remote((fr, ct)[k].at[rows], r1.at[k, me_zc], a_s.at[k, s], a_r.at[k, me_zc], dev)

    each(1, 16, lambda n: token_copy(0, n).start())
    for copy in own_w:
        copy.wait()

    def part(xx, half, ab):
        return wb.at[xx, pl.ds(half * 384 + ab * 192, 192)]

    def weight_copy(n):
        to_right = n in (0, 2, 4)
        xx = (x, x, x, x, x_left, x_right)[n]
        ab = (0, 1, 1, 0, 0, 1)[n]
        dev = (m, x_right if to_right else x_left)
        return remote(part(xx, c, ab), part(xx, c, ab), w_s.at[n], w_r.at[xx, ab], dev)

    for n in range(4):
        weight_copy(n).start()
    each(1, 16, lambda n: token_copy(1, n).start())

    def swap_copy(xx, ab):
        return remote(part(xx, c, ab), part(xx, c, ab), f_s.at[xx, ab], f_r.at[xx, ab], core_peer)

    def take_weights(xx, ab):
        arrive(part(xx, c, ab), w_r.at[xx, ab])
        swap_copy(xx, ab).start()

    order = feature_order_matrix()

    begin = runs[:, 0, :]
    end = begin + runs[:, 1, :]
    rows = []
    for i in range(4):
        place = (me_zc * 4 + x) * 16 + y * 4 + i
        inside = jnp.where((begin <= place) & (place < end), 1.0, 0.0)
        rows.append(jnp.sum(inside, axis=0, keepdims=True))
    rows = jnp.concatenate(rows + [jnp.zeros((4, 64), F32)], axis=0).astype(BF)
    columns = dot_nt(frame_order_matrix(), rows)
    for i in range(4):
        kept[pl.ds(64 * i, 64), :] = jnp.broadcast_to(columns[:, i : i + 1], (64, 128))
    first_of_pair = iota((64, 128), 1) < 64
    for p in range(2):
        keptw[p] = jnp.where(first_of_pair, kept[128 * p : 128 * p + 64, :], kept[128 * p + 64 : 128 * p + 128, :])

    def group_copy(k, n):
        yy, dev = y_peer(n)
        return remote(s2.at[k, yy], r2.at[k, :, y], b_s.at[k, yy], b_r.at[k, y], dev)

    def own_group(k):
        return pltpu.make_async_copy(s2.at[k, y], r2.at[k, :, y], l_s.at[4 + k])

    def regroup(k):
        each(1, 16, lambda n: arrive(r1.at[k, lax.rem(me_zc + n, 16)], a_r.at[k, lax.rem(me_zc + n, 16)]))
        own_rows(k).wait()
        s2[k] = dot(turn, r1[k].reshape(256, D)).astype(BF).reshape(4, 4, 16, D)
        for n in (1, 3, 2):
            group_copy(k, n).start()
        own_group(k).start()

    def grouped(k):
        for n in (1, 3, 2):
            yy = lax.rem(y + n, 4)
            arrive(r2.at[k, :, yy], b_r.at[k, yy])
        own_group(k).wait()

    regroup(0)
    take_weights(x_left, 0)
    weight_copy(4).start()
    take_weights(x_right, 1)
    weight_copy(5).start()
    grouped(0)

    tokens = r2[0].reshape(256, D).astype(F32)
    centre = jnp.mean(tokens, axis=-1, keepdims=True)
    shifted = tokens - centre
    inverse = lax.rsqrt(jnp.mean(shifted * shifted, axis=-1, keepdims=True) + EPS)
    standard = shifted * inverse
    std[...] = standard
    inv[...] = jnp.broadcast_to(inverse, (256, 128))
    gains = gain[...].reshape(1, D)
    normed = (standard * gains).astype(BF)
    nrm[...] = normed
    nt[...] = dot_nt(order, normed).astype(BF)
    ncot[...] = jnp.zeros((256, D), F32)
    br[...] = jnp.zeros((256, D), F32)

    lane = iota((64, 192), 1)
    head_mask = [(lane >= 64 * h) & (lane < 64 * h + 64) for h in range(3)]
    top_rows = iota((128, 192), 0) < 64
    nothing = jnp.zeros((128, 192), BF)

    def stack_heads(rows):
        return jnp.concatenate([jnp.where(hm, rows, jnp.zeros_like(rows)) for hm in head_mask], axis=0)

    def pick_heads(rows):
        return jnp.where(head_mask[0], rows[0:64], jnp.where(head_mask[1], rows[64:128], rows[128:192]))

    def only(rows, which):
        return jnp.where(top_rows, rows, nothing) if which == 0 else jnp.where(top_rows, nothing, rows)

    pairs = [slice(128 * p, 128 * p + 128) for p in range(2)]

    def forward_step(j):
        q, kk, v = [dot_nt(nrm[...], wb[j, 192 * n : 192 * n + 192, :]).astype(BF) for n in range(3)]
        qkv[j, 0], qkv[j, 1], qkv[j, 2] = q, kk, v
        kbd = [stack_heads(kk[64 * i : 64 * i + 64]) for i in range(4)]
        scores = [
            sum(dot_nt(kbd[2 * p + e], only(q[pairs[p]], e)) for e in range(2)) for p in range(2)
        ]
        vbd = [stack_heads(v[64 * i : 64 * i + 64]) for i in range(4)]
        weights = []
        for p in range(2):
            masked = jnp.where((keptw[p] > 0)[None], scores[p].reshape(3, 64, 128) * 0.125, -1000000000.0)
            top = jnp.max(masked, axis=1, keepdims=True)
            expo = jnp.exp(masked - top)
            weight = (expo / jnp.sum(expo, axis=1, keepdims=True)).reshape(192, 128)
            wts[j, p] = weight
            weights.append(weight.astype(BF))
        mixed = []
        for i in range(4):
            e = i % 2
            mixed.append(dot_tn(weights[i // 2], vbd[i])[64 * e : 64 * e + 64])
        mixed = jnp.concatenate(mixed, axis=0)
        mixed = jnp.where(kept[:, 0:1] > 0, mixed, 0.0).astype(BF)
        mx[j] = mixed
        br[...] += dot(mixed, wb[j, 576:768, :])

    forward_step(x)
    take_weights(x_left, 1)
    take_weights(x_right, 0)
    regroup(1)

    def forward_rest(n, carry):
        j = lax.rem(x + 2 * n + 1 - 3 * (n // 2), 4)

        @pl.when(n == 2)
        def _():
            take_weights(x_far, 0)
            take_weights(x_far, 1)

        arrive(part(j, 1 - c, 0), f_r.at[j, 0])
        arrive(part(j, 1 - c, 1), f_r.at[j, 1])
        forward_step(j)
        return carry

    lax.fori_loop(0, 3, forward_rest, 0)

    def pack_result(k, block):
        for xx in range(4):
            cols = slice(192 * xx, 192 * xx + 192)
            for i2 in range(2):
                rb[k, xx, i2] = jnp.concatenate(
                    [block[128 * i2 : 128 * i2 + 64, cols], block[128 * i2 + 64 : 128 * i2 + 128, cols]], axis=1
                ).reshape(4, 16, 384)

    def result_copy(k, n):
        yy, xx, dev = yx_peer(n)
        return remote(rb.at[k, xx, :, yy], t1.at[k, x, y], p_s.at[k, xx, yy], p_r.at[k, x, y], dev)

    def own_result(k):
        return pltpu.make_async_copy(rb.at[k, x, :, y], t1.at[k, x, y], l_s.at[6 + k])

    def send_result(k):
        each(1, 16, lambda n: result_copy(k, n).start())
        own_result(k).start()

    def place_copy(k, g, n):
        s, dev = zc_peer(n)
        return remote(t2.at[k, g, s], ot.at[k, me_zc, g], q_s.at[k, g, s], q_r.at[k, g, me_zc], dev)

    def own_place(k, g):
        return pltpu.make_async_copy(t2.at[k, g, me_zc], ot.at[k, me_zc, g], l_s.at[10 + 2 * k + g])

    def relay(k):
        def got(n):
            yy, xx, _ = yx_peer(n)
            arrive(t1.at[k, xx, yy], p_r.at[k, xx, yy])

        each(1, 16, got)
        own_result(k).wait()
        for g in range(2):
            t2[k, g] = dot(turn, t1[k, 2 * g : 2 * g + 2].reshape(256, 384)).astype(BF).reshape(16, 16, 384)
            each(1, 16, lambda n: place_copy(k, g, n).start())
            own_place(k, g).start()

    def placed(k, out):
        for g in range(2):
            own_place(k, g).wait()
            each(1, 16, lambda n: arrive(ot.at[k, lax.rem(me_zc + n, 16), g], q_r.at[k, g, lax.rem(me_zc + n, 16)]))
        unpair = unpair_matrix()
        for b in range(4):
            rows = ot[k, 4 * b : 4 * b + 4].reshape(128, 384)
            both = jnp.concatenate([rows[:, 0:192], rows[:, 192:384]], axis=0)
            out[:, 256 * b : 256 * b + 256] = dot_tn(both, unpair).astype(BF)

    pack_result(0, (r2[0].reshape(256, D).astype(F32) + br[...]).astype(BF))
    send_result(0)

    grouped(1)
    ctt[...] = dot_nt(order, r2[1].reshape(256, D)).astype(BF)

    def core_copy(jj):
        return remote(gb.at[jj, 1 - c], gc.at[jj], c_s.at[jj], c_r.at[jj], core_peer)

    def finish_core(jj):
        arrive(gc.at[jj], c_r.at[jj])
        hb[jj] = (gb[jj, c].astype(F32) + gc[jj].astype(F32)).astype(BF)

    left_cols, right_cols = pl.ds(0, 384), pl.ds(384, 384)

    def target(jj):
        return lax.rem(x + jj + 1, 4)

    def share_x(jj):
        return remote(hb.at[jj, :, left_cols], gx.at[x], x_s.at[jj], x_r.at[x], (m, target(jj)))

    def share_y(jj, n):
        yy, dev = y_peer(n)
        return remote(
            hb.at[jj, pl.ds(yy * 96, 96), right_cols], gy1.at[jj, y], y1_s.at[jj, yy], y1_r.at[jj, y], dev
        )

    def start_shares(jj):
        for n in (1, 3, 2):
            share_y(jj, n).start()

    def backward_step(jj, carry):
        j = target(jj)
        mc = dot_nt(r2[1].reshape(256, D), wb[j, 576:768, :])
        mc = jnp.where(kept[:, 0:1] > 0, mc, 0.0).astype(BF)
        q, kk, v = qkv[j, 0], qkv[j, 1], qkv[j, 2]
        vbd = [stack_heads(v[64 * i : 64 * i + 64]) for i in range(4)]
        kbd = [stack_heads(kk[64 * i : 64 * i + 64]) for i in range(4)]
        mcs = [only(mc[pairs[i // 2]], i % 2) for i in range(4)]
        qs = [only(q[pairs[i // 2]], i % 2) for i in range(4)]
        dws = [sum(dot_nt(vbd[2 * p + e], mcs[2 * p + e]) for e in range(2)) for p in range(2)]
        wbf = [wts[j, p].astype(BF) for p in range(2)]
        dv = [pick_heads(dot(wbf[i // 2], mcs[i])) for i in range(4)]
        dscores = []
        for p in range(2):
            weight = wts[j, p].reshape(3, 64, 128)
            dw = dws[p].reshape(3, 64, 128)
            inner = jnp.sum(dw * weight, axis=1, keepdims=True)
            dscores.append((weight * (dw - inner) * 0.125).astype(BF).reshape(192, 128))
        dq = []
        for i in range(4):
            e = i % 2
            dq.append(dot_tn(dscores[i // 2], kbd[i])[64 * e : 64 * e + 64])
        dk = [pick_heads(dot(dscores[i // 2], qs[i])) for i in range(4)]
        dq, dk, dv = [jnp.concatenate(part, axis=0).astype(BF) for part in (dq, dk, dv)]
        pcm[:, 0:192] = dq
        pcm[:, 192:384] = dk
        pcm[:, 384:576] = dv
        pcm[:, 576:768] = mx[j]
        low = iota((256, 256), 1) < 64
        tail = pcm[:, 512:768]
        tail_qkv = jnp.where(low, tail, jnp.zeros_like(tail))
        tail_mix = jnp.where(low, jnp.zeros_like(tail), tail)
        for h in range(2):
            rows = slice(384 * h, 384 * h + 384)
            gb[jj, h, :, 0:512] = dot(nt[rows, :], pcm[:, 0:512]).astype(BF)
            gb[jj, h, :, 512:768] = (dot(nt[rows, :], tail_qkv) + dot(ctt[rows, :], tail_mix)).astype(BF)
        core_copy(jj).start()
        ncot[...] += (
            dot(dq, wb[j, 0:192, :]) + dot(dk, wb[j, 192:384, :]) + dot(dv, wb[j, 384:576, :])
        )

        @pl.when(jj > 0)
        def _():
            finish_core(jj - 1)
            share_x(jj - 1).start()
            start_shares(jj - 1)

        @pl.when(jj == 1)
        def _():
            relay(0)

        return carry

    lax.fori_loop(0, 4, backward_step, 0)

    cotangent = ncot[...].astype(BF).astype(F32)
    standard = std[...]
    scaled = cotangent * gains
    mean_plain = jnp.mean(scaled, axis=-1, keepdims=True)
    mean_cross = jnp.mean(scaled * standard, axis=-1, keepdims=True)
    through = inv[:, 0:1] * (scaled - mean_plain - standard * mean_cross)
    pack_result(1, (r2[1].reshape(256, D).astype(F32) + through).astype(BF))
    send_result(1)

    gain_part = jnp.sum(cotangent * standard, axis=0, keepdims=True)
    vg[0] = jnp.concatenate(
        [gain_part[:, 192 * k : 192 * k + 192] for k in range(4)] + [jnp.zeros((4, 192), F32)], axis=0
    )
    gain_core = remote(vg.at[0], vgc, vc_s, vc_r, core_peer)
    gain_core.start()
    finish_core(3)
    start_shares(3)

    def share_x2(jj):
        return remote(hy1.at[jj], gx2.at[x], x2_s.at[jj], x2_r.at[x], (m, target(jj)))

    def sum_y1(jj):
        total = hb[jj, pl.ds(pl.multiple_of(y * 96, 16), 96), 384:768].astype(F32)
        for n in range(1, 4):
            yy = lax.rem(y + n, 4)
            arrive(gy1.at[jj, yy], y1_r.at[jj, yy])
            total = total + gy1[jj, yy].astype(F32)
        hy1[jj] = total.astype(BF)

    def sum_y1_send(jj):
        sum_y1(jj)
        share_x2(jj).start()

    each(0, 3, sum_y1_send)

    total = hb[3, :, 0:384].astype(F32)
    for n in range(1, 4):
        xx = lax.rem(x + n, 4)
        arrive(gx.at[xx], x_r.at[xx])
        total = total + gx[xx].astype(F32)
    hx[...] = total.astype(BF).reshape(4, 96, 384)

    def share_y2(n):
        yy, dev = y_peer(n)
        return remote(hx.at[yy], gy2.at[y], y2_s.at[yy], y2_r.at[y], dev)

    for n in (1, 3, 2):
        share_y2(n).start()

    arrive(vgc, vc_r)
    vg[1] = vg[0] + vgc[...]

    def gain_x(n):
        xx, dev = x_peer(n)
        return remote(vg.at[1], vgx.at[x], vx_s.at[xx], vx_r.at[x], dev)

    for n in range(1, 4):
        gain_x(n).start()

    relay(1)
    sum_y1(3)

    gain_total = vg[1]
    for n in range(1, 4):
        xx = lax.rem(x + n, 4)
        arrive(vgx.at[xx], vx_r.at[xx])
        gain_total = gain_total + vgx[xx]
    vg[2] = gain_total

    def gain_y(n):
        yy, dev = y_peer(n)
        return remote(vg.at[2], vgy.at[y], vy_s.at[yy], vy_r.at[y], dev)

    for n in range(1, 4):
        gain_y(n).start()

    left = hx[y].astype(F32)
    right = hy1[3].astype(F32)
    for n in range(1, 4):
        yy = lax.rem(y + n, 4)
        xx = lax.rem(x + n, 4)
        arrive(gy2.at[yy], y2_r.at[yy])
        arrive(gx2.at[xx], x2_r.at[xx])
        left = left + gy2[yy].astype(F32)
        right = right + gx2[xx].astype(F32)
    spread = spread_matrix()
    gzs[:, :, 0:384] = dot(spread, left.astype(BF)).astype(BF).reshape(8, 16, 384)
    gzs[:, :, 384:768] = dot(spread, right.astype(BF)).astype(BF).reshape(8, 16, 384)

    def grad_z(n):
        zz, dev = z_peer(n)
        return remote(gzs.at[zz], gz.at[z], z_s.at[zz], z_r.at[z], dev)

    for n in range(1, 8):
        grad_z(n).start()

    gain_total = vg[2]
    for n in range(1, 4):
        yy = lax.rem(y + n, 4)
        arrive(vgy.at[yy], vy_r.at[yy])
        gain_total = gain_total + vgy[yy]
    vg[3] = gain_total

    def gain_z(n):
        zz, dev = z_peer(n)
        return remote(vg.at[3], vgz.at[z], vz_s.at[zz], vz_r.at[z], dev)

    for n in range(1, 8):
        gain_z(n).start()

    placed(0, o_bo)

    total = gzs[z].astype(F32)
    gain_total = vg[3]
    for n in range(1, 8):
        zz = lax.rem(z + n, 8)
        arrive(gz.at[zz], z_r.at[zz])
        arrive(vgz.at[zz], vz_r.at[zz])
        total = total + gz[zz].astype(F32)
        gain_total = gain_total + vgz[zz]
    total = total[0:12]
    for n in range(3):
        o_gq[:, n, :] = total[:, 192 * n : 192 * n + 192].astype(BF)
    o_gp[...] = total[:, 576:768].astype(BF)
    o_gg[...] = jnp.sum(jnp.where(iota((8, 192), 0) == x, gain_total, 0.0), axis=0)

    placed(1, o_gi)

    def sent(n):
        for k in range(2):
            token_copy(k, n).wait_send()
            result_copy(k, n).wait_send()
            for g in range(2):
                place_copy(k, g, n).wait_send()

    each(1, 16, sent)
    for n in range(6):
        weight_copy(n).wait_send()
    for n in range(1, 4):
        xx = lax.rem(x + n, 4)
        swap_copy(xx, 0).wait_send()
        swap_copy(xx, 1).wait_send()
        group_copy(0, n).wait_send()
        group_copy(1, n).wait_send()
        gain_x(n).wait_send()
        share_y2(n).wait_send()
        gain_y(n).wait_send()

        def sent_y(jj):
            share_y(jj, n).wait_send()

        each(0, 4, sent_y)
    each(0, 4, lambda jj: core_copy(jj).wait_send())
    each(0, 3, lambda jj: share_x(jj).wait_send())
    each(0, 3, lambda jj: share_x2(jj).wait_send())
    for n in range(1, 8):
        grad_z(n).wait_send()
        gain_z(n).wait_send()
    gain_core.wait_send()


def body(frames_in, norm_gain, w_qkv, w_out, keep_runs, out_cotangent):
    v = lambda shape, dt=BF: pltpu.VMEM(shape, dt)
    dma = pltpu.SemaphoreType.DMA
    any_spec = pl.BlockSpec(memory_space=pl.ANY)
    vmem_spec = pl.BlockSpec(memory_space=pltpu.VMEM)
    block_out, grad_in, grad_qkv, grad_proj, grad_gain = pl.pallas_call(
        kernel,
        out_shape=(
            jax.ShapeDtypeStruct((192, 1024), BF),
            jax.ShapeDtypeStruct((192, 1024), BF),
            jax.ShapeDtypeStruct((12, 3, 192), BF),
            jax.ShapeDtypeStruct((12, 192), BF),
            jax.ShapeDtypeStruct((192,), F32),
        ),
        in_specs=[any_spec, any_spec, vmem_spec, any_spec, any_spec, vmem_spec],
        out_specs=(vmem_spec,) * 5,
        scratch_shapes=[
            v((2, 16, 16, D)),
            v((2, 4, 4, 16, D)),
            v((2, 4, 4, 16, D)),
            v((4, D, D)),
            v((256, D), F32),
            v((256, 128), F32),
            v((256, D)),
            v((D, 256)),
            v((D, 256)),
            v((256, D), F32),
            v((256, D), F32),
            v((256, 128), F32),
            v((2, 64, 128), F32),
            v((4, 3, 256, 192)),
            v((4, 2, 192, 128), F32),
            v((4, 256, 192)),
            v((256, D)),
            v((4, 2, 384, D)),
            v((4, 384, D)),
            v((4, 384, D)),
            v((4, 384, 384)),
            v((4, 4, 96, 384)),
            v((4, 96, 384)),
            v((4, 96, 384)),
            v((4, 96, 384)),
            v((4, 96, 384)),
            v((8, 16, D)),
            v((8, 16, D)),
            v((2, 4, 2, 4, 16, 384)),
            v((2, 4, 4, 2, 16, 384)),
            v((2, 2, 16, 16, 384)),
            v((2, 16, 2, 16, 384)),
            v((4, 8, 192), F32),
            v((8, 192), F32),
            v((4, 8, 192), F32),
            v((4, 8, 192), F32),
            v((8, 8, 192), F32),
            dma((2, 16)), dma((2, 16)),
            dma((2, 4)), dma((2, 4)),
            dma((6,)), dma((4, 2)),
            dma((4, 2)), dma((4, 2)),
            dma((4,)), dma((4,)),
            dma((4,)), dma((4,)),
            dma((4, 4)), dma((4, 4)),
            dma((4,)), dma((4,)),
            dma((4,)), dma((4,)),
            dma((8,)), dma((8,)),
            dma((2, 4, 4)), dma((2, 4, 4)),
            dma((2, 2, 16)), dma((2, 2, 16)),
            dma(()), dma(()),
            dma((4,)), dma((4,)),
            dma((4,)), dma((4,)),
            dma((8,)), dma((8,)),
            dma((14,)),
        ],
        compiler_params=pltpu.CompilerParams(
            collective_id=0, has_side_effects=True, vmem_limit_bytes=56 << 20
        ),
        cost_estimate=pl.CostEstimate(flops=5 * 10**9, bytes_accessed=10**7, transcendentals=200000),
        name="block",
    )(
        frames_in.reshape(1024, D),
        out_cotangent.reshape(1024, D),
        norm_gain,
        w_qkv.transpose(1, 2, 0).reshape(576, D),
        w_out,
        keep_runs.transpose(1, 2, 0),
    )
    return (
        block_out.T.reshape(1, 1024, 192),
        grad_in.T.reshape(1, 1024, 192),
        grad_qkv,
        grad_proj.T,
        grad_gain,
    )


def solution(mesh):
    in_specs = (
        P("tm", None, None),
        P(),
        P(None, None, "tensor"),
        P("tensor", None),
        P(),
        P("tm", None, None),
    )
    out_specs = (
        P("tm", None, "tensor"),
        P("tm", None, "tensor"),
        P("tm", None, "tensor"),
        P("tensor", "tm"),
        P("tensor"),
    )
    return jax.shard_map(body, mesh=mesh, in_specs=in_specs, out_specs=out_specs, check_vma=False)
```

```python
import jax
import jax.numpy as jnp
from jax import lax
from jax.experimental import pallas as pl
from jax.experimental.pallas import tpu as pltpu
from jax.sharding import PartitionSpec as P

MESH = pl.DeviceIdType.MESH
EARLY = 2
RELAY = 2
BF = jnp.bfloat16
F32 = jnp.float32
D = 768
EPS = 1e-05


def dot(a, b):
    return lax.dot_general(a, b, (((1,), (0,)), ((), ())), preferred_element_type=F32)


def dot_nt(a, b):
    return lax.dot_general(a, b, (((1,), (1,)), ((), ())), preferred_element_type=F32)


def dot_tn(a, b):
    return lax.dot_general(a, b, (((0,), (0,)), ((), ())), preferred_element_type=F32)


def iota(shape, axis):
    return lax.broadcasted_iota(jnp.int32, shape, axis)


def row_transpose_matrix():
    row = iota((256, 256), 0)
    col = iota((256, 256), 1)
    source = (row & 15) * 16 + (row >> 4)
    return jnp.where(col == source, 1.0, 0.0).astype(BF)


def feature_order_matrix():
    row = iota((D, 1), 0)
    core = (row >= 384).astype(jnp.int32)
    rest = row - 384 * core
    y = sum((rest >= 96 * k).astype(jnp.int32) for k in range(1, 4))
    rest = rest - 96 * y
    z = sum((rest >= 12 * k).astype(jnp.int32) for k in range(1, 8))
    rest = rest - 12 * z
    source = 12 * (z * 8 + y * 2 + core) + rest
    return jnp.where(iota((D, D), 1) == source, 1.0, 0.0).astype(BF)


def spread_matrix():
    row = iota((128, 96), 0)
    col = iota((128, 96), 1)
    inner = row & 15
    return jnp.where((inner < 12) & (col == (row >> 4) * 12 + inner), 1.0, 0.0).astype(BF)


def frame_order_matrix():
    row = iota((64, 64), 0)
    source = ((row >> 1) & 7) * 8 + (row >> 4) * 2 + (row & 1)
    return jnp.where(iota((64, 64), 1) == source, 1.0, 0.0).astype(BF)


def unpair_matrix():
    row = iota((256, 256), 0)
    col = iota((256, 256), 1)
    return jnp.where(col == (row & 127) * 2 + (row >> 7), 1.0, 0.0).astype(BF)


def kernel(
    fr, ct, gain, wq, wo, runs,
    ot, o_gr, o_gg,
    r1, s2, r2, wb, std, inv, nrm, nt, ctt, ncot, br, kept, qkv, wts, mx, mcs, dp, pcm,
    gb, gc, hb, gx, gy1, hy1, gx2, hx, gy2, gzs, gz,
    rb, t1, t2, vg, vgc, vgx, vgy, vgz,
    a_s, a_r, b_s, b_r, w_s, w_r, f_s, f_r, c_s, c_r, x_s, x_r, y1_s, y1_r, x2_s, x2_r,
    y2_s, y2_r, z_s, z_r, p_s, p_r, q_s, q_r, vc_s, vc_r, vx_s, vx_r, vy_s, vy_r, vz_s, vz_r, l_s,
):
    m = lax.axis_index("tm")
    x = lax.axis_index("tensor")
    z = m // 8
    y = lax.rem(m // 2, 4)
    c = lax.rem(m, 2)
    me_zc = z * 2 + c

    def zc_peer(n):
        near = (n + 1) // 2
        k = near + (1 - lax.rem(n, 2)) * (16 - 2 * near)
        s = lax.rem(me_zc + k, 16)
        return s, ((s // 2) * 8 + y * 2 + lax.rem(s, 2), x)

    def yx_peer(k):
        q = lax.rem(x * 4 + y + k, 16)
        yy, xx = lax.rem(q, 4), q // 4
        return yy, xx, (z * 8 + yy * 2 + c, xx)

    def x_peer(k):
        xx = lax.rem(x + k, 4)
        return xx, (m, xx)

    def y_peer(k):
        yy = lax.rem(y + k, 4)
        return yy, (z * 8 + yy * 2 + c, x)

    def z_peer(k):
        zz = lax.rem(z + k, 8)
        return zz, (zz * 8 + y * 2 + c, x)

    core_peer = (z * 8 + y * 2 + (1 - c), x)
    x_right, x_left, x_far = lax.rem(x + 1, 4), lax.rem(x + 3, 4), lax.rem(x + 2, 4)

    def remote(src, dst, ss, rs, dev):
        return pltpu.make_async_remote_copy(
            src_ref=src, dst_ref=dst, send_sem=ss, recv_sem=rs, device_id=dev, device_id_type=MESH
        )

    def arrive(dst, rs):
        remote(dst, dst, l_s.at[9], rs, core_peer).wait_recv()

    def each(first, last, body):
        def step(k, carry):
            body(k)
            return carry
        lax.fori_loop(first, last, step, 0)

    barrier = pltpu.get_barrier_semaphore()

    def greet(k):
        pl.semaphore_signal(barrier, inc=1, device_id=zc_peer(k)[1], device_id_type=MESH)
        pl.semaphore_signal(barrier, inc=1, device_id=yx_peer(k)[2], device_id_type=MESH)

    each(1, 16, greet)

    own_w = [
        pltpu.make_async_copy(wq, wb.at[x, pl.ds(0, 576)], l_s.at[0]),
        pltpu.make_async_copy(wo, wb.at[x, pl.ds(576, 192)], l_s.at[3]),
    ]
    for copy in own_w:
        copy.start()

    def own_rows(k):
        ref = (fr, ct)[k]
        return pltpu.make_async_copy(
            ref.at[pl.ds((me_zc * 4 + x) * 16, 16)], r1.at[k, me_zc], l_s.at[1 + k]
        )

    own_rows(0).start()
    own_rows(1).start()
    turn = row_transpose_matrix()
    pl.semaphore_wait(barrier, 30)

    def token_copy(k, n):
        s, dev = zc_peer(n)
        rows = pl.ds((s * 4 + x) * 16, 16)
        return remote((fr, ct)[k].at[rows], r1.at[k, me_zc], a_s.at[k, s], a_r.at[k, me_zc], dev)

    each(1, 16, lambda n: token_copy(0, n).start())
    for copy in own_w:
        copy.wait()

    def part(xx, half, ab):
        return wb.at[xx, pl.ds(half * 384 + ab * 192, 192)]

    def weight_copy(n):
        to_right = n in (0, 2, 4)
        xx = (x, x, x, x, x_left, x_right)[n]
        ab = (0, 1, 1, 0, 0, 1)[n]
        dev = (m, x_right if to_right else x_left)
        return remote(part(xx, c, ab), part(xx, c, ab), w_s.at[n], w_r.at[xx, ab], dev)

    for n in range(4):
        weight_copy(n).start()
    each(1, 16, lambda n: token_copy(1, n).start())

    def swap_copy(xx, ab):
        return remote(part(xx, c, ab), part(xx, c, ab), f_s.at[xx, ab], f_r.at[xx, ab], core_peer)

    def take_weights(xx, ab):
        arrive(part(xx, c, ab), w_r.at[xx, ab])
        swap_copy(xx, ab).start()

    order = feature_order_matrix()

    begin = runs[:, 0, :]
    end = begin + runs[:, 1, :]
    rows = []
    for i in range(4):
        place = (me_zc * 4 + x) * 16 + y * 4 + i
        inside = jnp.where((begin <= place) & (place < end), 1.0, 0.0)
        rows.append(jnp.sum(inside, axis=0, keepdims=True))
    rows = jnp.concatenate(rows + [jnp.zeros((4, 64), F32)], axis=0).astype(BF)
    columns = dot_nt(frame_order_matrix(), rows)
    for i in range(4):
        kept[pl.ds(64 * i, 64), :] = jnp.broadcast_to(columns[:, i : i + 1], (64, 128))
    def group_copy(k, n):
        yy, dev = y_peer(n)
        return remote(s2.at[k, yy], r2.at[k, :, y], b_s.at[k, yy], b_r.at[k, y], dev)

    def own_group(k):
        return pltpu.make_async_copy(s2.at[k, y], r2.at[k, :, y], l_s.at[4 + k])

    def regroup(k):
        each(1, 16, lambda n: arrive(r1.at[k, lax.rem(me_zc + n, 16)], a_r.at[k, lax.rem(me_zc + n, 16)]))
        own_rows(k).wait()
        s2[k] = dot(turn, r1[k].reshape(256, D)).astype(BF).reshape(4, 4, 16, D)
        for n in (1, 3, 2):
            group_copy(k, n).start()
        own_group(k).start()

    def grouped(k):
        for n in (1, 3, 2):
            yy = lax.rem(y + n, 4)
            arrive(r2.at[k, :, yy], b_r.at[k, yy])
        own_group(k).wait()

    regroup(0)
    take_weights(x_left, 0)
    weight_copy(4).start()
    take_weights(x_right, 1)
    weight_copy(5).start()
    grouped(0)

    tokens = r2[0].reshape(256, D).astype(F32)
    centre = jnp.mean(tokens, axis=-1, keepdims=True)
    shifted = tokens - centre
    inverse = lax.rsqrt(jnp.mean(shifted * shifted, axis=-1, keepdims=True) + EPS)
    standard = shifted * inverse
    std[...] = standard
    inv[...] = jnp.broadcast_to(inverse, (256, 128))
    gains = gain[...].reshape(1, D)
    normed = (standard * gains).astype(BF)
    nrm[...] = normed
    nt[...] = dot_nt(order, normed).astype(BF)
    ncot[...] = jnp.zeros((256, D), F32)
    br[...] = jnp.zeros((256, D), F32)

    lane = iota((64, 192), 1)
    head_mask = [(lane >= 64 * h) & (lane < 64 * h + 64) for h in range(3)]
    head_ones = [jnp.where(hm, 1.0, 0.0).astype(BF) for hm in head_mask]

    def stack_heads(rows):
        return jnp.concatenate([rows * ones for ones in head_ones], axis=0)

    def pick_heads(rows):
        return jnp.where(head_mask[0], rows[0:64], jnp.where(head_mask[1], rows[64:128], rows[128:192]))

    spots = [slice(64 * i, 64 * i + 64) for i in range(4)]

    def forward_step(j):
        for n in range(3):
            qkv[j, n] = dot_nt(nrm[...], wb[j, 192 * n : 192 * n + 192, :]).astype(BF)
        keep = [kept[spot, 0:1] > 0 for spot in spots]
        scores = [dot_nt(qkv[j, 1, spot], stack_heads(qkv[j, 0, spot])) for spot in spots]
        rounded = []
        for i in range(4):
            masked = jnp.where(keep[i], scores[i] * 0.125, -1000000000.0)
            expo = jnp.exp(masked - jnp.max(masked, axis=0, keepdims=True))
            weight = expo / jnp.sum(expo, axis=0, keepdims=True)
            wts[j, i] = weight
            rounded.append(weight.astype(BF))
        crossed = [dot_tn(rounded[i], qkv[j, 2, spot]) for i, spot in enumerate(spots)]
        mixed = [jnp.where(keep[i], pick_heads(crossed[i]), 0.0) for i in range(4)]
        mx[j] = jnp.concatenate(mixed, axis=0).astype(BF)
        br[...] += dot(mx[j], wb[j, 576:768, :])

    forward_step(x)
    take_weights(x_left, 1)
    take_weights(x_right, 0)
    regroup(1)

    def forward_rest(n, carry):
        j = lax.rem(x + 2 * n + 1 - 3 * (n // 2), 4)

        @pl.when(n == 2)
        def _():
            take_weights(x_far, 0)
            take_weights(x_far, 1)

        arrive(part(j, 1 - c, 0), f_r.at[j, 0])
        arrive(part(j, 1 - c, 1), f_r.at[j, 1])
        forward_step(j)
        return carry

    lax.fori_loop(0, 3, forward_rest, 0)

    def pack_result(k, block):
        for xx in range(4):
            cols = slice(192 * xx, 192 * xx + 192)
            for i2 in range(2):
                rb[k, xx, i2] = jnp.concatenate(
                    [block[128 * i2 : 128 * i2 + 64, cols], block[128 * i2 + 64 : 128 * i2 + 128, cols]], axis=1
                ).reshape(4, 16, 384)

    def result_copy(k, n):
        yy, xx, dev = yx_peer(n)
        return remote(rb.at[k, xx, :, yy], t1.at[k, x, y], p_s.at[k, xx, yy], p_r.at[k, x, y], dev)

    def own_result(k):
        return pltpu.make_async_copy(rb.at[k, x, :, y], t1.at[k, x, y], l_s.at[6 + k])

    def send_result(k):
        each(1, 16, lambda n: result_copy(k, n).start())
        own_result(k).start()

    def place_copy(k, g, n):
        s, dev = zc_peer(n)
        return remote(t2.at[k, g, s], ot.at[k, me_zc, g], q_s.at[k, g, s], q_r.at[k, g, me_zc], dev)

    def own_place(k, g):
        return pltpu.make_async_copy(t2.at[k, g, me_zc], ot.at[k, me_zc, g], l_s.at[10 + 2 * k + g])

    def relay(k):
        def got(n):
            yy, xx, _ = yx_peer(n)
            arrive(t1.at[k, xx, yy], p_r.at[k, xx, yy])

        each(1, 16, got)
        own_result(k).wait()
        for g in range(2):
            t2[k, g] = dot(turn, t1[k, 2 * g : 2 * g + 2].reshape(256, 384)).astype(BF).reshape(16, 16, 384)
            each(1, 16, lambda n: place_copy(k, g, n).start())
            own_place(k, g).start()

    def placed(k):
        for g in range(2):
            own_place(k, g).wait()
            each(1, 16, lambda n: arrive(ot.at[k, lax.rem(me_zc + n, 16), g], q_r.at[k, g, lax.rem(me_zc + n, 16)]))

    pack_result(0, (r2[0].reshape(256, D).astype(F32) + br[...]).astype(BF))
    send_result(0)

    grouped(1)
    ctt[...] = dot_nt(order, r2[1].reshape(256, D)).astype(BF)

    def core_copy(jj):
        return remote(gb.at[jj, 1 - c], gc.at[jj], c_s.at[jj], c_r.at[jj], core_peer)

    def finish_core(jj):
        arrive(gc.at[jj], c_r.at[jj])
        hb[jj] = (gb[jj, c].astype(F32) + gc[jj].astype(F32)).astype(BF)

    left_cols, right_cols = pl.ds(0, 384), pl.ds(384, 384)

    def target(jj):
        return lax.rem(x + jj + 1, 4)

    def share_x(jj):
        return remote(hb.at[jj, :, left_cols], gx.at[x], x_s.at[jj], x_r.at[x], (m, target(jj)))

    def share_y(jj, n):
        yy, dev = y_peer(n)
        return remote(
            hb.at[jj, pl.ds(yy * 96, 96), right_cols], gy1.at[jj, y], y1_s.at[jj, yy], y1_r.at[jj, y], dev
        )

    def start_shares(jj):
        for n in (1, 3, 2):
            share_y(jj, n).start()

    def backward_step(jj, carry):
        j = target(jj)
        mc = dot_nt(r2[1].reshape(256, D), wb[j, 576:768, :])
        mcs[...] = jnp.where(kept[:, 0:1] > 0, mc, 0.0).astype(BF)
        mcb = [stack_heads(mcs[spot]) for spot in spots]
        dws = [dot_nt(qkv[j, 2, spot], mcb[i]) for i, spot in enumerate(spots)]
        dv = [dot(wts[j, i].astype(BF), mcb[i]) for i in range(4)]
        dscores = []
        for i in range(4):
            weight = wts[j, i]
            inner = jnp.sum(dws[i] * weight, axis=0, keepdims=True)
            dscores.append((weight * (dws[i] - inner) * 0.125).astype(BF))
        dk = [dot(dscores[i], stack_heads(qkv[j, 0, spot])) for i, spot in enumerate(spots)]
        dq = [pick_heads(dot_tn(dscores[i], qkv[j, 1, spot])) for i, spot in enumerate(spots)]
        for n, pieces in enumerate((dq, dk, dv)):
            dp[n] = jnp.concatenate(pieces, axis=0).astype(BF)
        for n in range(3):
            pcm[:, 192 * n : 192 * n + 192] = dp[n]
        pcm[:, 576:768] = mx[j]
        low = iota((256, 256), 1) < 64
        tail = pcm[:, 512:768]
        tail_qkv = jnp.where(low, tail, jnp.zeros_like(tail))
        tail_mix = jnp.where(low, jnp.zeros_like(tail), tail)
        for h in range(2):
            rows = slice(384 * h, 384 * h + 384)
            gb[jj, h, :, 0:512] = dot(nt[rows, :], pcm[:, 0:512]).astype(BF)
            gb[jj, h, :, 512:768] = (dot(nt[rows, :], tail_qkv) + dot(ctt[rows, :], tail_mix)).astype(BF)
        core_copy(jj).start()
        ncot[...] += (
            dot(dp[0], wb[j, 0:192, :]) + dot(dp[1], wb[j, 192:384, :]) + dot(dp[2], wb[j, 384:576, :])
        )

        @pl.when(jj > 0)
        def _():
            finish_core(jj - 1)

        @pl.when((jj > 0) & (jj < EARLY + 1))
        def _():
            share_x(jj - 1).start()
            start_shares(jj - 1)

        @pl.when(jj == RELAY)
        def _():
            relay(0)

        return carry

    lax.fori_loop(0, 4, backward_step, 0)

    cotangent = ncot[...].astype(BF).astype(F32)
    standard = std[...]
    scaled = cotangent * gains
    mean_plain = jnp.mean(scaled, axis=-1, keepdims=True)
    mean_cross = jnp.mean(scaled * standard, axis=-1, keepdims=True)
    through = inv[:, 0:1] * (scaled - mean_plain - standard * mean_cross)
    pack_result(1, (r2[1].reshape(256, D).astype(F32) + through).astype(BF))
    send_result(1)
    for jj in range(EARLY, 3):
        share_x(jj).start()
        start_shares(jj)

    gain_part = jnp.sum(cotangent * standard, axis=0, keepdims=True)
    vg[0] = jnp.concatenate(
        [gain_part[:, 192 * k : 192 * k + 192] for k in range(4)] + [jnp.zeros((4, 192), F32)], axis=0
    )
    gain_core = remote(vg.at[0], vgc, vc_s, vc_r, core_peer)
    gain_core.start()
    finish_core(3)
    start_shares(3)

    def share_x2(jj):
        return remote(hy1.at[jj], gx2.at[x], x2_s.at[jj], x2_r.at[x], (m, target(jj)))

    def sum_y1(jj):
        total = hb[jj, pl.ds(pl.multiple_of(y * 96, 16), 96), 384:768].astype(F32)
        for n in range(1, 4):
            yy = lax.rem(y + n, 4)
            arrive(gy1.at[jj, yy], y1_r.at[jj, yy])
            total = total + gy1[jj, yy].astype(F32)
        hy1[jj] = total.astype(BF)

    def sum_y1_send(jj):
        sum_y1(jj)
        share_x2(jj).start()

    relay(1)
    each(0, 3, sum_y1_send)

    total = hb[3, :, 0:384].astype(F32)
    for n in range(1, 4):
        xx = lax.rem(x + n, 4)
        arrive(gx.at[xx], x_r.at[xx])
        total = total + gx[xx].astype(F32)
    hx[...] = total.astype(BF).reshape(4, 96, 384)

    def share_y2(n):
        yy, dev = y_peer(n)
        return remote(hx.at[yy], gy2.at[y], y2_s.at[yy], y2_r.at[y], dev)

    for n in (1, 3, 2):
        share_y2(n).start()

    arrive(vgc, vc_r)
    vg[1] = vg[0] + vgc[...]

    def gain_x(n):
        xx, dev = x_peer(n)
        return remote(vg.at[1], vgx.at[x], vx_s.at[xx], vx_r.at[x], dev)

    for n in range(1, 4):
        gain_x(n).start()

    sum_y1(3)

    gain_total = vg[1]
    for n in range(1, 4):
        xx = lax.rem(x + n, 4)
        arrive(vgx.at[xx], vx_r.at[xx])
        gain_total = gain_total + vgx[xx]
    vg[2] = gain_total

    def gain_y(n):
        yy, dev = y_peer(n)
        return remote(vg.at[2], vgy.at[y], vy_s.at[yy], vy_r.at[y], dev)

    for n in range(1, 4):
        gain_y(n).start()

    left = hx[y].astype(F32)
    right = hy1[3].astype(F32)
    for n in range(1, 4):
        yy = lax.rem(y + n, 4)
        xx = lax.rem(x + n, 4)
        arrive(gy2.at[yy], y2_r.at[yy])
        arrive(gx2.at[xx], x2_r.at[xx])
        left = left + gy2[yy].astype(F32)
        right = right + gx2[xx].astype(F32)
    spread = spread_matrix()
    gzs[:, :, 0:384] = dot(spread, left.astype(BF)).astype(BF).reshape(8, 16, 384)
    gzs[:, :, 384:768] = dot(spread, right.astype(BF)).astype(BF).reshape(8, 16, 384)

    def grad_z(n):
        zz, dev = z_peer(n)
        return remote(gzs.at[zz], gz.at[z], z_s.at[zz], z_r.at[z], dev)

    for n in range(1, 8):
        grad_z(n).start()

    gain_total = vg[2]
    for n in range(1, 4):
        yy = lax.rem(y + n, 4)
        arrive(vgy.at[yy], vy_r.at[yy])
        gain_total = gain_total + vgy[yy]
    vg[3] = gain_total

    def gain_z(n):
        zz, dev = z_peer(n)
        return remote(vg.at[3], vgz.at[z], vz_s.at[zz], vz_r.at[z], dev)

    for n in range(1, 8):
        gain_z(n).start()


    total = gzs[z].astype(F32)
    gain_total = vg[3]
    for n in range(1, 8):
        zz = lax.rem(z + n, 8)
        arrive(gz.at[zz], z_r.at[zz])
        arrive(vgz.at[zz], vz_r.at[zz])
        total = total + gz[zz].astype(F32)
        gain_total = gain_total + vgz[zz]
    o_gr[...] = total
    o_gg[...] = jnp.broadcast_to(
        jnp.sum(jnp.where(iota((8, 192), 0) == x, gain_total, 0.0), axis=0, keepdims=True), (8, 192)
    )

    placed(0)
    placed(1)

    def sent(n):
        for k in range(2):
            token_copy(k, n).wait_send()
            result_copy(k, n).wait_send()
            for g in range(2):
                place_copy(k, g, n).wait_send()

    each(1, 16, sent)
    for n in range(6):
        weight_copy(n).wait_send()
    for n in range(1, 4):
        xx = lax.rem(x + n, 4)
        swap_copy(xx, 0).wait_send()
        swap_copy(xx, 1).wait_send()
        group_copy(0, n).wait_send()
        group_copy(1, n).wait_send()
        gain_x(n).wait_send()
        share_y2(n).wait_send()
        gain_y(n).wait_send()

        def sent_y(jj):
            share_y(jj, n).wait_send()

        each(0, 4, sent_y)
    each(0, 4, lambda jj: core_copy(jj).wait_send())
    each(0, 3, lambda jj: share_x(jj).wait_send())
    each(0, 3, lambda jj: share_x2(jj).wait_send())
    for n in range(1, 8):
        grad_z(n).wait_send()
        gain_z(n).wait_send()
    gain_core.wait_send()


def finish(ot, gr, gg, o_bo, o_gi, o_gq, o_gp, o_gg):
    unpair = unpair_matrix()
    for k, out in enumerate((o_bo, o_gi)):
        for b in range(4):
            rows = ot[k, 4 * b : 4 * b + 4].reshape(128, 384)
            both = jnp.concatenate([rows[:, 0:192], rows[:, 192:384]], axis=0)
            out[:, 256 * b : 256 * b + 256] = dot_tn(both, unpair).astype(BF)
    total = gr[0:12, :]
    for n in range(3):
        o_gq[:, n, :] = total[:, 192 * n : 192 * n + 192].astype(BF)
    o_gp[...] = total[:, 576:768].astype(BF)
    o_gg[...] = gg[0, :]


def body(frames_in, norm_gain, w_qkv, w_out, keep_runs, out_cotangent):
    v = lambda shape, dt=BF: pltpu.VMEM(shape, dt)
    dma = pltpu.SemaphoreType.DMA
    any_spec = pl.BlockSpec(memory_space=pl.ANY)
    vmem_spec = pl.BlockSpec(memory_space=pltpu.VMEM)
    placed, grads, gain_sum = pl.pallas_call(
        kernel,
        out_shape=(
            jax.ShapeDtypeStruct((2, 16, 2, 16, 384), BF),
            jax.ShapeDtypeStruct((16, D), F32),
            jax.ShapeDtypeStruct((8, 192), F32),
        ),
        in_specs=[any_spec, any_spec, vmem_spec, any_spec, any_spec, vmem_spec],
        out_specs=(any_spec, vmem_spec, vmem_spec),
        scratch_shapes=[
            v((2, 16, 16, D)),
            v((2, 4, 4, 16, D)),
            v((2, 4, 4, 16, D)),
            v((4, D, D)),
            v((256, D), F32),
            v((256, 128), F32),
            v((256, D)),
            v((D, 256)),
            v((D, 256)),
            v((256, D), F32),
            v((256, D), F32),
            v((256, 128), F32),
            v((4, 3, 256, 192)),
            v((4, 4, 64, 192), F32),
            v((4, 256, 192)),
            v((256, 192)),
            v((3, 256, 192)),
            v((256, D)),
            v((4, 2, 384, D)),
            v((4, 384, D)),
            v((4, 384, D)),
            v((4, 384, 384)),
            v((4, 4, 96, 384)),
            v((4, 96, 384)),
            v((4, 96, 384)),
            v((4, 96, 384)),
            v((4, 96, 384)),
            v((8, 16, D)),
            v((8, 16, D)),
            v((2, 4, 2, 4, 16, 384)),
            v((2, 4, 4, 2, 16, 384)),
            v((2, 2, 16, 16, 384)),
            v((4, 8, 192), F32),
            v((8, 192), F32),
            v((4, 8, 192), F32),
            v((4, 8, 192), F32),
            v((8, 8, 192), F32),
            dma((2, 16)), dma((2, 16)),
            dma((2, 4)), dma((2, 4)),
            dma((6,)), dma((4, 2)),
            dma((4, 2)), dma((4, 2)),
            dma((4,)), dma((4,)),
            dma((4,)), dma((4,)),
            dma((4, 4)), dma((4, 4)),
            dma((4,)), dma((4,)),
            dma((4,)), dma((4,)),
            dma((8,)), dma((8,)),
            dma((2, 4, 4)), dma((2, 4, 4)),
            dma((2, 2, 16)), dma((2, 2, 16)),
            dma(()), dma(()),
            dma((4,)), dma((4,)),
            dma((4,)), dma((4,)),
            dma((8,)), dma((8,)),
            dma((14,)),
        ],
        compiler_params=pltpu.CompilerParams(
            collective_id=0, has_side_effects=True, vmem_limit_bytes=56 << 20
        ),
        cost_estimate=pl.CostEstimate(flops=5 * 10**9, bytes_accessed=10**7, transcendentals=200000),
        name="block",
    )(
        frames_in.reshape(1024, D),
        out_cotangent.reshape(1024, D),
        norm_gain,
        w_qkv.transpose(1, 2, 0).reshape(576, D),
        w_out,
        keep_runs.transpose(1, 2, 0),
    )
    block_out, grad_in, grad_qkv, grad_proj, grad_gain = pl.pallas_call(
        finish,
        out_shape=(
            jax.ShapeDtypeStruct((192, 1024), BF),
            jax.ShapeDtypeStruct((192, 1024), BF),
            jax.ShapeDtypeStruct((12, 3, 192), BF),
            jax.ShapeDtypeStruct((12, 192), BF),
            jax.ShapeDtypeStruct((192,), F32),
        ),
        in_specs=[vmem_spec] * 3,
        out_specs=(vmem_spec,) * 5,
        compiler_params=pltpu.CompilerParams(vmem_limit_bytes=60 << 20),
        cost_estimate=pl.CostEstimate(flops=4 * 10**8, bytes_accessed=3 * 10**6, transcendentals=0),
        name="finish",
    )(placed, grads, gain_sum)
    return (
        block_out.T.reshape(1, 1024, 192),
        grad_in.T.reshape(1, 1024, 192),
        grad_qkv,
        grad_proj.T,
        grad_gain,
    )


def solution(mesh):
    in_specs = (
        P("tm", None, None),
        P(),
        P(None, None, "tensor"),
        P("tensor", None),
        P(),
        P("tm", None, None),
    )
    out_specs = (
        P("tm", None, "tensor"),
        P("tm", None, "tensor"),
        P("tm", None, "tensor"),
        P("tensor", "tm"),
        P("tensor"),
    )
    return jax.shard_map(body, mesh=mesh, in_specs=in_specs, out_specs=out_specs, check_vma=False)
```

```python
import jax
import jax.numpy as jnp
from jax import lax
from jax.experimental import pallas as pl
from jax.experimental.pallas import tpu as pltpu
from jax.sharding import PartitionSpec as P

MESH = pl.DeviceIdType.MESH
EARLY = 2
RELAY = 2
BF = jnp.bfloat16
F32 = jnp.float32
D = 768
EPS = 1e-05


def dot(a, b):
    return lax.dot_general(a, b, (((1,), (0,)), ((), ())), preferred_element_type=F32)


def dot_nt(a, b):
    return lax.dot_general(a, b, (((1,), (1,)), ((), ())), preferred_element_type=F32)


def dot_tn(a, b):
    return lax.dot_general(a, b, (((0,), (0,)), ((), ())), preferred_element_type=F32)


def iota(shape, axis):
    return lax.broadcasted_iota(jnp.int32, shape, axis)


def row_transpose_matrix():
    row = iota((256, 256), 0)
    col = iota((256, 256), 1)
    source = (row & 15) * 16 + (row >> 4)
    return jnp.where(col == source, 1.0, 0.0).astype(BF)


def feature_order_matrix():
    row = iota((D, 1), 0)
    core = (row >= 384).astype(jnp.int32)
    rest = row - 384 * core
    y = sum((rest >= 96 * k).astype(jnp.int32) for k in range(1, 4))
    rest = rest - 96 * y
    z = sum((rest >= 12 * k).astype(jnp.int32) for k in range(1, 8))
    rest = rest - 12 * z
    source = 12 * (z * 8 + y * 2 + core) + rest
    return jnp.where(iota((D, D), 1) == source, 1.0, 0.0).astype(BF)


def spread_matrix():
    row = iota((128, 96), 0)
    col = iota((128, 96), 1)
    inner = row & 15
    return jnp.where((inner < 12) & (col == (row >> 4) * 12 + inner), 1.0, 0.0).astype(BF)


def frame_order_matrix():
    row = iota((64, 64), 0)
    source = ((row >> 1) & 7) * 8 + (row >> 4) * 2 + (row & 1)
    return jnp.where(iota((64, 64), 1) == source, 1.0, 0.0).astype(BF)


def unpair_matrix():
    row = iota((256, 256), 0)
    col = iota((256, 256), 1)
    return jnp.where(col == (row & 127) * 2 + (row >> 7), 1.0, 0.0).astype(BF)


def kernel(
    fr, ct, gain, wq, wo, runs,
    ot, o_gr, o_gg,
    r1, s2, u2, u3, u4, r2, wb, std, inv, nrm, nt, ctt, ncot, br, kept, qkv, wts, mx, mcs, dp, pcm,
    gb, gc, hb, gx, gy1, hy1, gx2, hx, gy2, gzs, gz,
    rb, t1, t2, vg, vgc, vgx, vgy, vgz,
    a_s, a_r, b_s, b_r, w_s, w_r, f_s, f_r, c_s, c_r, x_s, x_r, y1_s, y1_r, x2_s, x2_r,
    y2_s, y2_r, z_s, z_r, p_s, p_r, q_s, q_r, vc_s, vc_r, vx_s, vx_r, vy_s, vy_r, vz_s, vz_r, l_s,
):
    m = lax.axis_index("tm")
    x = lax.axis_index("tensor")
    z = m // 8
    y = lax.rem(m // 2, 4)
    c = lax.rem(m, 2)
    me_zc = z * 2 + c

    def zc_peer(n):
        near = (n + 1) // 2
        k = near + (1 - lax.rem(n, 2)) * (16 - 2 * near)
        s = lax.rem(me_zc + k, 16)
        return s, ((s // 2) * 8 + y * 2 + lax.rem(s, 2), x)

    def yx_peer(k):
        q = lax.rem(x * 4 + y + k, 16)
        yy, xx = lax.rem(q, 4), q // 4
        return yy, xx, (z * 8 + yy * 2 + c, xx)

    def x_peer(k):
        xx = lax.rem(x + k, 4)
        return xx, (m, xx)

    def y_peer(k):
        yy = lax.rem(y + k, 4)
        return yy, (z * 8 + yy * 2 + c, x)

    def z_peer(k):
        zz = lax.rem(z + k, 8)
        return zz, (zz * 8 + y * 2 + c, x)

    core_peer = (z * 8 + y * 2 + (1 - c), x)
    x_right, x_left, x_far = lax.rem(x + 1, 4), lax.rem(x + 3, 4), lax.rem(x + 2, 4)

    def remote(src, dst, ss, rs, dev):
        return pltpu.make_async_remote_copy(
            src_ref=src, dst_ref=dst, send_sem=ss, recv_sem=rs, device_id=dev, device_id_type=MESH
        )

    def arrive(dst, rs):
        remote(dst, dst, l_s.at[9], rs, core_peer).wait_recv()

    def each(first, last, body):
        def step(k, carry):
            body(k)
            return carry
        lax.fori_loop(first, last, step, 0)

    barrier = pltpu.get_barrier_semaphore()

    def greet(k):
        pl.semaphore_signal(barrier, inc=1, device_id=zc_peer(k)[1], device_id_type=MESH)
        pl.semaphore_signal(barrier, inc=1, device_id=yx_peer(k)[2], device_id_type=MESH)

    each(1, 16, greet)

    own_w = [
        pltpu.make_async_copy(wq, wb.at[x, pl.ds(0, 576)], l_s.at[0]),
        pltpu.make_async_copy(wo, wb.at[x, pl.ds(576, 192)], l_s.at[3]),
    ]
    for copy in own_w:
        copy.start()

    own_rows = pltpu.make_async_copy(
        fr.at[pl.ds((me_zc * 4 + x) * 16, 16)], r1.at[0, me_zc], l_s.at[1]
    )
    own_rows.start()
    own_share = pltpu.make_async_copy(ct.at[:, x], r1.at[1], l_s.at[14])
    own_share.start()
    turn = row_transpose_matrix()
    own_share.wait()
    s2[1] = dot(turn, r1[1].reshape(256, D)).astype(BF).reshape(4, 4, 16, D)
    pl.semaphore_wait(barrier, 30)

    def token_copy(k, n):
        s, dev = zc_peer(n)
        if k == 0:
            source, landing = fr.at[pl.ds((s * 4 + x) * 16, 16)], r1.at[0, me_zc]
        else:
            source, landing = u3.at[s], u4.at[me_zc]
        return remote(source, landing, a_s.at[k, s], a_r.at[k, me_zc], dev)

    def group_copy(k, n):
        yy, dev = y_peer(n)
        landing = r2.at[0, :, y] if k == 0 else u2.at[:, y]
        return remote(s2.at[k, yy], landing, b_s.at[k, yy], b_r.at[k, y], dev)

    def own_group(k):
        return pltpu.make_async_copy(s2.at[k, y], r2.at[0, :, y] if k == 0 else u2.at[:, y], l_s.at[4 + k])

    def send_groups(k):
        for n in (1, 3, 2):
            group_copy(k, n).start()
        own_group(k).start()

    def grouped(k):
        for n in (1, 3, 2):
            yy = lax.rem(y + n, 4)
            arrive(r2.at[0, :, yy] if k == 0 else u2.at[:, yy], b_r.at[k, yy])
        own_group(k).wait()

    each(1, 16, lambda n: token_copy(0, n).start())
    send_groups(1)
    for copy in own_w:
        copy.wait()

    def part(xx, half, ab):
        return wb.at[xx, pl.ds(half * 384 + ab * 192, 192)]

    def weight_copy(n):
        to_right = n in (0, 2, 4)
        xx = (x, x, x, x, x_left, x_right)[n]
        ab = (0, 1, 1, 0, 0, 1)[n]
        dev = (m, x_right if to_right else x_left)
        return remote(part(xx, c, ab), part(xx, c, ab), w_s.at[n], w_r.at[xx, ab], dev)

    for n in range(4):
        weight_copy(n).start()
    def swap_copy(xx, ab):
        return remote(part(xx, c, ab), part(xx, c, ab), f_s.at[xx, ab], f_r.at[xx, ab], core_peer)

    def take_weights(xx, ab):
        arrive(part(xx, c, ab), w_r.at[xx, ab])
        swap_copy(xx, ab).start()

    order = feature_order_matrix()

    begin = runs[:, 0, :]
    end = begin + runs[:, 1, :]
    rows = []
    for i in range(4):
        place = (me_zc * 4 + x) * 16 + y * 4 + i
        inside = jnp.where((begin <= place) & (place < end), 1.0, 0.0)
        rows.append(jnp.sum(inside, axis=0, keepdims=True))
    rows = jnp.concatenate(rows + [jnp.zeros((4, 64), F32)], axis=0).astype(BF)
    columns = dot_nt(frame_order_matrix(), rows)
    for i in range(4):
        kept[pl.ds(64 * i, 64), :] = jnp.broadcast_to(columns[:, i : i + 1], (64, 128))
    own_column = pltpu.make_async_copy(u3.at[me_zc], u4.at[me_zc], l_s.at[2])

    def pass_cotangent():
        grouped(1)
        u3[...] = dot(turn, u2[...].reshape(256, D)).astype(BF).reshape(16, 16, D)
        each(1, 16, lambda n: token_copy(1, n).start())
        own_column.start()

    def take_cotangent():
        each(1, 16, lambda n: arrive(u4.at[lax.rem(me_zc + n, 16)], a_r.at[1, lax.rem(me_zc + n, 16)]))
        own_column.wait()
        r2[1] = dot(turn, u4[...].reshape(256, D)).astype(BF).reshape(4, 4, 16, D)

    pass_cotangent()
    each(1, 16, lambda n: arrive(r1.at[0, lax.rem(me_zc + n, 16)], a_r.at[0, lax.rem(me_zc + n, 16)]))
    own_rows.wait()
    s2[0] = dot(turn, r1[0].reshape(256, D)).astype(BF).reshape(4, 4, 16, D)
    send_groups(0)
    take_weights(x_left, 0)
    weight_copy(4).start()
    take_weights(x_right, 1)
    weight_copy(5).start()
    grouped(0)

    tokens = r2[0].reshape(256, D).astype(F32)
    centre = jnp.mean(tokens, axis=-1, keepdims=True)
    shifted = tokens - centre
    inverse = lax.rsqrt(jnp.mean(shifted * shifted, axis=-1, keepdims=True) + EPS)
    standard = shifted * inverse
    std[...] = standard
    inv[...] = jnp.broadcast_to(inverse, (256, 128))
    gains = gain[...].reshape(1, D)
    normed = (standard * gains).astype(BF)
    nrm[...] = normed
    nt[...] = dot_nt(order, normed).astype(BF)
    ncot[...] = jnp.zeros((256, D), F32)
    br[...] = jnp.zeros((256, D), F32)

    lane = iota((64, 192), 1)
    head_mask = [(lane >= 64 * h) & (lane < 64 * h + 64) for h in range(3)]
    head_ones = [jnp.where(hm, 1.0, 0.0).astype(BF) for hm in head_mask]

    def stack_heads(rows):
        return jnp.concatenate([rows * ones for ones in head_ones], axis=0)

    def pick_heads(rows):
        return jnp.where(head_mask[0], rows[0:64], jnp.where(head_mask[1], rows[64:128], rows[128:192]))

    spots = [slice(64 * i, 64 * i + 64) for i in range(4)]

    def forward_step(j):
        for n in range(3):
            qkv[j, n] = dot_nt(nrm[...], wb[j, 192 * n : 192 * n + 192, :]).astype(BF)
        keep = [kept[spot, 0:1] > 0 for spot in spots]
        scores = [dot_nt(qkv[j, 1, spot], stack_heads(qkv[j, 0, spot])) for spot in spots]
        rounded = []
        for i in range(4):
            masked = jnp.where(keep[i], scores[i] * 0.125, -1000000000.0)
            expo = jnp.exp(masked - jnp.max(masked, axis=0, keepdims=True))
            weight = expo / jnp.sum(expo, axis=0, keepdims=True)
            wts[j, i] = weight
            rounded.append(weight.astype(BF))
        crossed = [dot_tn(rounded[i], qkv[j, 2, spot]) for i, spot in enumerate(spots)]
        mixed = [jnp.where(keep[i], pick_heads(crossed[i]), 0.0) for i in range(4)]
        mx[j] = jnp.concatenate(mixed, axis=0).astype(BF)
        br[...] += dot(mx[j], wb[j, 576:768, :])

    forward_step(x)
    take_weights(x_left, 1)
    take_weights(x_right, 0)

    def forward_rest(n, carry):
        j = lax.rem(x + 2 * n + 1 - 3 * (n // 2), 4)

        @pl.when(n == 2)
        def _():
            take_weights(x_far, 0)
            take_weights(x_far, 1)

        arrive(part(j, 1 - c, 0), f_r.at[j, 0])
        arrive(part(j, 1 - c, 1), f_r.at[j, 1])
        forward_step(j)
        return carry

    lax.fori_loop(0, 3, forward_rest, 0)

    def pack_result(k, block):
        for xx in range(4):
            cols = slice(192 * xx, 192 * xx + 192)
            for i2 in range(2):
                rb[k, xx, i2] = jnp.concatenate(
                    [block[128 * i2 : 128 * i2 + 64, cols], block[128 * i2 + 64 : 128 * i2 + 128, cols]], axis=1
                ).reshape(4, 16, 384)

    def result_copy(k, n):
        yy, xx, dev = yx_peer(n)
        return remote(rb.at[k, xx, :, yy], t1.at[k, x, y], p_s.at[k, xx, yy], p_r.at[k, x, y], dev)

    def own_result(k):
        return pltpu.make_async_copy(rb.at[k, x, :, y], t1.at[k, x, y], l_s.at[6 + k])

    def send_result(k):
        each(1, 16, lambda n: result_copy(k, n).start())
        own_result(k).start()

    def place_copy(k, g, n):
        s, dev = zc_peer(n)
        return remote(t2.at[k, g, s], ot.at[k, me_zc, g], q_s.at[k, g, s], q_r.at[k, g, me_zc], dev)

    def own_place(k, g):
        return pltpu.make_async_copy(t2.at[k, g, me_zc], ot.at[k, me_zc, g], l_s.at[10 + 2 * k + g])

    def relay(k):
        def got(n):
            yy, xx, _ = yx_peer(n)
            arrive(t1.at[k, xx, yy], p_r.at[k, xx, yy])

        each(1, 16, got)
        own_result(k).wait()
        for g in range(2):
            t2[k, g] = dot(turn, t1[k, 2 * g : 2 * g + 2].reshape(256, 384)).astype(BF).reshape(16, 16, 384)
            each(1, 16, lambda n: place_copy(k, g, n).start())
            own_place(k, g).start()

    def placed(k):
        for g in range(2):
            own_place(k, g).wait()
            each(1, 16, lambda n: arrive(ot.at[k, lax.rem(me_zc + n, 16), g], q_r.at[k, g, lax.rem(me_zc + n, 16)]))

    pack_result(0, (r2[0].reshape(256, D).astype(F32) + br[...]).astype(BF))
    send_result(0)

    take_cotangent()
    ctt[...] = dot_nt(order, r2[1].reshape(256, D)).astype(BF)

    def core_copy(jj):
        return remote(gb.at[jj, 1 - c], gc.at[jj], c_s.at[jj], c_r.at[jj], core_peer)

    def finish_core(jj):
        arrive(gc.at[jj], c_r.at[jj])
        hb[jj] = (gb[jj, c].astype(F32) + gc[jj].astype(F32)).astype(BF)

    left_cols, right_cols = pl.ds(0, 384), pl.ds(384, 384)

    def target(jj):
        return lax.rem(x + jj + 1, 4)

    def share_x(jj):
        return remote(hb.at[jj, :, left_cols], gx.at[x], x_s.at[jj], x_r.at[x], (m, target(jj)))

    def share_y(jj, n):
        yy, dev = y_peer(n)
        return remote(
            hb.at[jj, pl.ds(yy * 96, 96), right_cols], gy1.at[jj, y], y1_s.at[jj, yy], y1_r.at[jj, y], dev
        )

    def start_shares(jj):
        for n in (1, 3, 2):
            share_y(jj, n).start()

    def backward_step(jj, carry):
        j = target(jj)
        mc = dot_nt(r2[1].reshape(256, D), wb[j, 576:768, :])
        mcs[...] = jnp.where(kept[:, 0:1] > 0, mc, 0.0).astype(BF)
        mcb = [stack_heads(mcs[spot]) for spot in spots]
        dws = [dot_nt(qkv[j, 2, spot], mcb[i]) for i, spot in enumerate(spots)]
        dv = [dot(wts[j, i].astype(BF), mcb[i]) for i in range(4)]
        dscores = []
        for i in range(4):
            weight = wts[j, i]
            inner = jnp.sum(dws[i] * weight, axis=0, keepdims=True)
            dscores.append((weight * (dws[i] - inner) * 0.125).astype(BF))
        dk = [dot(dscores[i], stack_heads(qkv[j, 0, spot])) for i, spot in enumerate(spots)]
        dq = [pick_heads(dot_tn(dscores[i], qkv[j, 1, spot])) for i, spot in enumerate(spots)]
        for n, pieces in enumerate((dq, dk, dv)):
            dp[n] = jnp.concatenate(pieces, axis=0).astype(BF)
        for n in range(3):
            pcm[:, 192 * n : 192 * n + 192] = dp[n]
        pcm[:, 576:768] = mx[j]
        low = iota((256, 256), 1) < 64
        tail = pcm[:, 512:768]
        tail_qkv = jnp.where(low, tail, jnp.zeros_like(tail))
        tail_mix = jnp.where(low, jnp.zeros_like(tail), tail)
        for h in range(2):
            rows = slice(384 * h, 384 * h + 384)
            gb[jj, h, :, 0:512] = dot(nt[rows, :], pcm[:, 0:512]).astype(BF)
            gb[jj, h, :, 512:768] = (dot(nt[rows, :], tail_qkv) + dot(ctt[rows, :], tail_mix)).astype(BF)
        core_copy(jj).start()
        ncot[...] += (
            dot(dp[0], wb[j, 0:192, :]) + dot(dp[1], wb[j, 192:384, :]) + dot(dp[2], wb[j, 384:576, :])
        )

        @pl.when(jj > 0)
        def _():
            finish_core(jj - 1)

        @pl.when((jj > 0) & (jj < EARLY + 1))
        def _():
            share_x(jj - 1).start()
            start_shares(jj - 1)

        @pl.when(jj == RELAY)
        def _():
            relay(0)

        return carry

    lax.fori_loop(0, 4, backward_step, 0)

    cotangent = ncot[...].astype(BF).astype(F32)
    standard = std[...]
    scaled = cotangent * gains
    mean_plain = jnp.mean(scaled, axis=-1, keepdims=True)
    mean_cross = jnp.mean(scaled * standard, axis=-1, keepdims=True)
    through = inv[:, 0:1] * (scaled - mean_plain - standard * mean_cross)
    pack_result(1, (r2[1].reshape(256, D).astype(F32) + through).astype(BF))
    send_result(1)
    for jj in range(EARLY, 3):
        share_x(jj).start()
        start_shares(jj)

    gain_part = jnp.sum(cotangent * standard, axis=0, keepdims=True)
    vg[0] = jnp.concatenate(
        [gain_part[:, 192 * k : 192 * k + 192] for k in range(4)] + [jnp.zeros((4, 192), F32)], axis=0
    )
    gain_core = remote(vg.at[0], vgc, vc_s, vc_r, core_peer)
    gain_core.start()
    finish_core(3)
    start_shares(3)

    def share_x2(jj):
        return remote(hy1.at[jj], gx2.at[x], x2_s.at[jj], x2_r.at[x], (m, target(jj)))

    def sum_y1(jj):
        total = hb[jj, pl.ds(pl.multiple_of(y * 96, 16), 96), 384:768].astype(F32)
        for n in range(1, 4):
            yy = lax.rem(y + n, 4)
            arrive(gy1.at[jj, yy], y1_r.at[jj, yy])
            total = total + gy1[jj, yy].astype(F32)
        hy1[jj] = total.astype(BF)

    def sum_y1_send(jj):
        sum_y1(jj)
        share_x2(jj).start()

    relay(1)
    each(0, 3, sum_y1_send)

    total = hb[3, :, 0:384].astype(F32)
    for n in range(1, 4):
        xx = lax.rem(x + n, 4)
        arrive(gx.at[xx], x_r.at[xx])
        total = total + gx[xx].astype(F32)
    hx[...] = total.astype(BF).reshape(4, 96, 384)

    def share_y2(n):
        yy, dev = y_peer(n)
        return remote(hx.at[yy], gy2.at[y], y2_s.at[yy], y2_r.at[y], dev)

    for n in (1, 3, 2):
        share_y2(n).start()

    arrive(vgc, vc_r)
    vg[1] = vg[0] + vgc[...]

    def gain_x(n):
        xx, dev = x_peer(n)
        return remote(vg.at[1], vgx.at[x], vx_s.at[xx], vx_r.at[x], dev)

    for n in range(1, 4):
        gain_x(n).start()

    sum_y1(3)

    gain_total = vg[1]
    for n in range(1, 4):
        xx = lax.rem(x + n, 4)
        arrive(vgx.at[xx], vx_r.at[xx])
        gain_total = gain_total + vgx[xx]
    vg[2] = gain_total

    def gain_y(n):
        yy, dev = y_peer(n)
        return remote(vg.at[2], vgy.at[y], vy_s.at[yy], vy_r.at[y], dev)

    for n in range(1, 4):
        gain_y(n).start()

    left = hx[y].astype(F32)
    right = hy1[3].astype(F32)
    for n in range(1, 4):
        yy = lax.rem(y + n, 4)
        xx = lax.rem(x + n, 4)
        arrive(gy2.at[yy], y2_r.at[yy])
        arrive(gx2.at[xx], x2_r.at[xx])
        left = left + gy2[yy].astype(F32)
        right = right + gx2[xx].astype(F32)
    spread = spread_matrix()
    gzs[:, :, 0:384] = dot(spread, left.astype(BF)).astype(BF).reshape(8, 16, 384)
    gzs[:, :, 384:768] = dot(spread, right.astype(BF)).astype(BF).reshape(8, 16, 384)

    def grad_z(n):
        zz, dev = z_peer(n)
        return remote(gzs.at[zz], gz.at[z], z_s.at[zz], z_r.at[z], dev)

    for n in range(1, 8):
        grad_z(n).start()

    gain_total = vg[2]
    for n in range(1, 4):
        yy = lax.rem(y + n, 4)
        arrive(vgy.at[yy], vy_r.at[yy])
        gain_total = gain_total + vgy[yy]
    vg[3] = gain_total

    def gain_z(n):
        zz, dev = z_peer(n)
        return remote(vg.at[3], vgz.at[z], vz_s.at[zz], vz_r.at[z], dev)

    for n in range(1, 8):
        gain_z(n).start()


    total = gzs[z].astype(F32)
    gain_total = vg[3]
    for n in range(1, 8):
        zz = lax.rem(z + n, 8)
        arrive(gz.at[zz], z_r.at[zz])
        arrive(vgz.at[zz], vz_r.at[zz])
        total = total + gz[zz].astype(F32)
        gain_total = gain_total + vgz[zz]
    o_gr[...] = total
    o_gg[...] = jnp.broadcast_to(
        jnp.sum(jnp.where(iota((8, 192), 0) == x, gain_total, 0.0), axis=0, keepdims=True), (8, 192)
    )

    placed(0)
    placed(1)

    def sent(n):
        for k in range(2):
            token_copy(k, n).wait_send()
            result_copy(k, n).wait_send()
            for g in range(2):
                place_copy(k, g, n).wait_send()

    each(1, 16, sent)
    for n in range(6):
        weight_copy(n).wait_send()
    for n in range(1, 4):
        xx = lax.rem(x + n, 4)
        swap_copy(xx, 0).wait_send()
        swap_copy(xx, 1).wait_send()
        group_copy(0, n).wait_send()
        group_copy(1, n).wait_send()
        gain_x(n).wait_send()
        share_y2(n).wait_send()
        gain_y(n).wait_send()

        def sent_y(jj):
            share_y(jj, n).wait_send()

        each(0, 4, sent_y)
    each(0, 4, lambda jj: core_copy(jj).wait_send())
    each(0, 3, lambda jj: share_x(jj).wait_send())
    each(0, 3, lambda jj: share_x2(jj).wait_send())
    for n in range(1, 8):
        grad_z(n).wait_send()
        gain_z(n).wait_send()
    gain_core.wait_send()


def finish(ot, gr, gg, o_bo, o_gi, o_gq, o_gp, o_gg):
    unpair = unpair_matrix()
    for k, out in enumerate((o_bo, o_gi)):
        for b in range(4):
            rows = ot[k, 4 * b : 4 * b + 4].reshape(128, 384)
            both = jnp.concatenate([rows[:, 0:192], rows[:, 192:384]], axis=0)
            out[:, 256 * b : 256 * b + 256] = dot_tn(both, unpair).astype(BF)
    total = gr[0:12, :]
    for n in range(3):
        o_gq[:, n, :] = total[:, 192 * n : 192 * n + 192].astype(BF)
    o_gp[...] = total[:, 576:768].astype(BF)
    o_gg[...] = gg[0, :]


def body(frames_in, norm_gain, w_qkv, w_out, keep_runs, out_cotangent):
    v = lambda shape, dt=BF: pltpu.VMEM(shape, dt)
    dma = pltpu.SemaphoreType.DMA
    any_spec = pl.BlockSpec(memory_space=pl.ANY)
    vmem_spec = pl.BlockSpec(memory_space=pltpu.VMEM)
    placed, grads, gain_sum = pl.pallas_call(
        kernel,
        out_shape=(
            jax.ShapeDtypeStruct((2, 16, 2, 16, 384), BF),
            jax.ShapeDtypeStruct((16, D), F32),
            jax.ShapeDtypeStruct((8, 192), F32),
        ),
        in_specs=[any_spec, any_spec, vmem_spec, any_spec, any_spec, vmem_spec],
        out_specs=(any_spec, vmem_spec, vmem_spec),
        scratch_shapes=[
            v((2, 16, 16, D)),
            v((2, 4, 4, 16, D)),
            v((4, 4, 16, D)),
            v((16, 16, D)),
            v((16, 16, D)),
            v((2, 4, 4, 16, D)),
            v((4, D, D)),
            v((256, D), F32),
            v((256, 128), F32),
            v((256, D)),
            v((D, 256)),
            v((D, 256)),
            v((256, D), F32),
            v((256, D), F32),
            v((256, 128), F32),
            v((4, 3, 256, 192)),
            v((4, 4, 64, 192), F32),
            v((4, 256, 192)),
            v((256, 192)),
            v((3, 256, 192)),
            v((256, D)),
            v((4, 2, 384, D)),
            v((4, 384, D)),
            v((4, 384, D)),
            v((4, 384, 384)),
            v((4, 4, 96, 384)),
            v((4, 96, 384)),
            v((4, 96, 384)),
            v((4, 96, 384)),
            v((4, 96, 384)),
            v((8, 16, D)),
            v((8, 16, D)),
            v((2, 4, 2, 4, 16, 384)),
            v((2, 4, 4, 2, 16, 384)),
            v((2, 2, 16, 16, 384)),
            v((4, 8, 192), F32),
            v((8, 192), F32),
            v((4, 8, 192), F32),
            v((4, 8, 192), F32),
            v((8, 8, 192), F32),
            dma((2, 16)), dma((2, 16)),
            dma((2, 4)), dma((2, 4)),
            dma((6,)), dma((4, 2)),
            dma((4, 2)), dma((4, 2)),
            dma((4,)), dma((4,)),
            dma((4,)), dma((4,)),
            dma((4, 4)), dma((4, 4)),
            dma((4,)), dma((4,)),
            dma((4,)), dma((4,)),
            dma((8,)), dma((8,)),
            dma((2, 4, 4)), dma((2, 4, 4)),
            dma((2, 2, 16)), dma((2, 2, 16)),
            dma(()), dma(()),
            dma((4,)), dma((4,)),
            dma((4,)), dma((4,)),
            dma((8,)), dma((8,)),
            dma((15,)),
        ],
        compiler_params=pltpu.CompilerParams(
            collective_id=0, has_side_effects=True, vmem_limit_bytes=56 << 20
        ),
        cost_estimate=pl.CostEstimate(flops=5 * 10**9, bytes_accessed=10**7, transcendentals=200000),
        name="block",
    )(
        frames_in.reshape(1024, D),
        out_cotangent.reshape(16, 4, 16, D),
        norm_gain,
        w_qkv.transpose(1, 2, 0).reshape(576, D),
        w_out,
        keep_runs.transpose(1, 2, 0),
    )
    block_out, grad_in, grad_qkv, grad_proj, grad_gain = pl.pallas_call(
        finish,
        out_shape=(
            jax.ShapeDtypeStruct((192, 1024), BF),
            jax.ShapeDtypeStruct((192, 1024), BF),
            jax.ShapeDtypeStruct((12, 3, 192), BF),
            jax.ShapeDtypeStruct((12, 192), BF),
            jax.ShapeDtypeStruct((192,), F32),
        ),
        in_specs=[vmem_spec] * 3,
        out_specs=(vmem_spec,) * 5,
        compiler_params=pltpu.CompilerParams(vmem_limit_bytes=60 << 20),
        cost_estimate=pl.CostEstimate(flops=4 * 10**8, bytes_accessed=3 * 10**6, transcendentals=0),
        name="finish",
    )(placed, grads, gain_sum)
    return (
        block_out.T.reshape(1, 1024, 192),
        grad_in.T.reshape(1, 1024, 192),
        grad_qkv,
        grad_proj.T,
        grad_gain,
    )


def solution(mesh):
    in_specs = (
        P("tm", None, None),
        P(),
        P(None, None, "tensor"),
        P("tensor", None),
        P(),
        P("tm", None, None),
    )
    out_specs = (
        P("tm", None, "tensor"),
        P("tm", None, "tensor"),
        P("tm", None, "tensor"),
        P("tensor", "tm"),
        P("tensor"),
    )
    return jax.shard_map(body, mesh=mesh, in_specs=in_specs, out_specs=out_specs, check_vma=False)
```

```python
import jax
import jax.numpy as jnp
from jax import lax
from jax.experimental import pallas as pl
from jax.experimental.pallas import tpu as pltpu
from jax.sharding import PartitionSpec as P

MESH = pl.DeviceIdType.MESH
EARLY = 2
RELAY = 2
BF = jnp.bfloat16
F32 = jnp.float32
D = 768
EPS = 1e-05


def dot(a, b):
    return lax.dot_general(a, b, (((1,), (0,)), ((), ())), preferred_element_type=F32)


def dot_nt(a, b):
    return lax.dot_general(a, b, (((1,), (1,)), ((), ())), preferred_element_type=F32)


def dot_tn(a, b):
    return lax.dot_general(a, b, (((0,), (0,)), ((), ())), preferred_element_type=F32)


def iota(shape, axis):
    return lax.broadcasted_iota(jnp.int32, shape, axis)


def row_transpose_matrix():
    row = iota((256, 256), 0)
    col = iota((256, 256), 1)
    source = (row & 15) * 16 + (row >> 4)
    return jnp.where(col == source, 1.0, 0.0).astype(BF)


def feature_order_matrix():
    row = iota((D, 1), 0)
    core = (row >= 384).astype(jnp.int32)
    rest = row - 384 * core
    y = sum((rest >= 96 * k).astype(jnp.int32) for k in range(1, 4))
    rest = rest - 96 * y
    z = sum((rest >= 12 * k).astype(jnp.int32) for k in range(1, 8))
    rest = rest - 12 * z
    source = 12 * (z * 8 + y * 2 + core) + rest
    return jnp.where(iota((D, D), 1) == source, 1.0, 0.0).astype(BF)


def spread_matrix():
    row = iota((128, 96), 0)
    col = iota((128, 96), 1)
    inner = row & 15
    return jnp.where((inner < 12) & (col == (row >> 4) * 12 + inner), 1.0, 0.0).astype(BF)


def frame_order_matrix():
    row = iota((64, 64), 0)
    source = ((row >> 1) & 7) * 8 + (row >> 4) * 2 + (row & 1)
    return jnp.where(iota((64, 64), 1) == source, 1.0, 0.0).astype(BF)


def unpair_matrix():
    row = iota((256, 256), 0)
    col = iota((256, 256), 1)
    return jnp.where(col == (row & 127) * 2 + (row >> 7), 1.0, 0.0).astype(BF)


def kernel(
    fr, ct, gain, wq, wo, runs,
    ot, o_gr, o_gg,
    r1, s2, u2, u3, u4, r2, wb, std, inv, nrm, nt, ctt, ncot, br, kept, qkv, wts, mx, mcs, dp, pcm,
    gb, gc, hb, gx, gy1, hy1, gx2, hx, gy2, gzs, gz,
    rb, t1, t2, vg, vgc, vgx, vgy, vgz,
    a_s, a_r, b_s, b_r, w_s, w_r, f_s, f_r, c_s, c_r, x_s, x_r, y1_s, y1_r, x2_s, x2_r,
    y2_s, y2_r, z_s, z_r, p_s, p_r, q_s, q_r, vc_s, vc_r, vx_s, vx_r, vy_s, vy_r, vz_s, vz_r, l_s,
):
    m = lax.axis_index("tm")
    x = lax.axis_index("tensor")
    z = m // 8
    y = lax.rem(m // 2, 4)
    c = lax.rem(m, 2)
    me_zc = z * 2 + c

    def zc_peer(n):
        near = (n + 1) // 2
        k = near + (1 - lax.rem(n, 2)) * (16 - 2 * near)
        s = lax.rem(me_zc + k, 16)
        return s, ((s // 2) * 8 + y * 2 + lax.rem(s, 2), x)

    def yx_peer(k):
        q = lax.rem(x * 4 + y + k, 16)
        yy, xx = lax.rem(q, 4), q // 4
        return yy, xx, (z * 8 + yy * 2 + c, xx)

    def x_peer(k):
        xx = lax.rem(x + k, 4)
        return xx, (m, xx)

    def y_peer(k):
        yy = lax.rem(y + k, 4)
        return yy, (z * 8 + yy * 2 + c, x)

    def z_peer(k):
        zz = lax.rem(z + k, 8)
        return zz, (zz * 8 + y * 2 + c, x)

    core_peer = (z * 8 + y * 2 + (1 - c), x)
    x_right, x_left, x_far = lax.rem(x + 1, 4), lax.rem(x + 3, 4), lax.rem(x + 2, 4)

    def remote(src, dst, ss, rs, dev):
        return pltpu.make_async_remote_copy(
            src_ref=src, dst_ref=dst, send_sem=ss, recv_sem=rs, device_id=dev, device_id_type=MESH
        )

    def arrive(dst, rs):
        remote(dst, dst, l_s.at[9], rs, core_peer).wait_recv()

    def each(first, last, body):
        def step(k, carry):
            body(k)
            return carry
        lax.fori_loop(first, last, step, 0)

    barrier = pltpu.get_barrier_semaphore()

    def greet(k):
        pl.semaphore_signal(barrier, inc=1, device_id=zc_peer(k)[1], device_id_type=MESH)
        pl.semaphore_signal(barrier, inc=1, device_id=yx_peer(k)[2], device_id_type=MESH)

    each(1, 16, greet)

    own_w = [
        pltpu.make_async_copy(wq, wb.at[x, pl.ds(0, 576)], l_s.at[0]),
        pltpu.make_async_copy(wo, wb.at[x, pl.ds(576, 192)], l_s.at[3]),
    ]
    for copy in own_w:
        copy.start()

    own_rows = pltpu.make_async_copy(
        fr.at[pl.ds((me_zc * 4 + x) * 16, 16)], r1.at[0, me_zc], l_s.at[1]
    )
    own_rows.start()
    own_share = pltpu.make_async_copy(ct.at[:, x], r1.at[1], l_s.at[14])
    own_share.start()
    turn = row_transpose_matrix()
    own_share.wait()
    s2[1] = dot(turn, r1[1].reshape(256, D)).astype(BF).reshape(4, 4, 16, D)
    pl.semaphore_wait(barrier, 30)

    def token_copy(k, n):
        s, dev = zc_peer(n)
        if k == 0:
            source, landing = fr.at[pl.ds((s * 4 + x) * 16, 16)], r1.at[0, me_zc]
        else:
            source, landing = u3.at[s], u4.at[me_zc]
        return remote(source, landing, a_s.at[k, s], a_r.at[k, me_zc], dev)

    def group_copy(k, n):
        yy, dev = y_peer(n)
        landing = r2.at[0, :, y] if k == 0 else u2.at[:, y]
        return remote(s2.at[k, yy], landing, b_s.at[k, yy], b_r.at[k, y], dev)

    def own_group(k):
        return pltpu.make_async_copy(s2.at[k, y], r2.at[0, :, y] if k == 0 else u2.at[:, y], l_s.at[4 + k])

    def send_groups(k):
        for n in (1, 3, 2):
            group_copy(k, n).start()
        own_group(k).start()

    def grouped(k):
        for n in (1, 3, 2):
            yy = lax.rem(y + n, 4)
            arrive(r2.at[0, :, yy] if k == 0 else u2.at[:, yy], b_r.at[k, yy])
        own_group(k).wait()

    each(1, 16, lambda n: token_copy(0, n).start())
    send_groups(1)
    for copy in own_w:
        copy.wait()

    def part(xx, half, ab):
        return wb.at[xx, pl.ds(half * 384 + ab * 192, 192)]

    def weight_copy(n):
        to_right = n in (0, 2, 4)
        xx = (x, x, x, x, x_left, x_right)[n]
        ab = (0, 1, 1, 0, 0, 1)[n]
        dev = (m, x_right if to_right else x_left)
        return remote(part(xx, c, ab), part(xx, c, ab), w_s.at[n], w_r.at[xx, ab], dev)

    for n in range(4):
        weight_copy(n).start()
    def swap_copy(xx, ab):
        return remote(part(xx, c, ab), part(xx, c, ab), f_s.at[xx, ab], f_r.at[xx, ab], core_peer)

    def take_weights(xx, ab):
        arrive(part(xx, c, ab), w_r.at[xx, ab])
        swap_copy(xx, ab).start()

    order = feature_order_matrix()

    begin = runs[:, 0, :]
    end = begin + runs[:, 1, :]
    rows = []
    for i in range(4):
        place = (me_zc * 4 + x) * 16 + y * 4 + i
        inside = jnp.where((begin <= place) & (place < end), 1.0, 0.0)
        rows.append(jnp.sum(inside, axis=0, keepdims=True))
    rows = jnp.concatenate(rows + [jnp.zeros((4, 64), F32)], axis=0).astype(BF)
    columns = dot_nt(frame_order_matrix(), rows)
    for i in range(4):
        kept[pl.ds(64 * i, 64), :] = jnp.broadcast_to(columns[:, i : i + 1], (64, 128))
    own_column = pltpu.make_async_copy(u3.at[me_zc], u4.at[me_zc], l_s.at[2])

    def pass_cotangent():
        grouped(1)
        u3[...] = dot(turn, u2[...].reshape(256, D)).astype(BF).reshape(16, 16, D)
        each(1, 16, lambda n: token_copy(1, n).start())
        own_column.start()

    def take_cotangent():
        each(1, 16, lambda n: arrive(u4.at[lax.rem(me_zc + n, 16)], a_r.at[1, lax.rem(me_zc + n, 16)]))
        own_column.wait()
        r2[1] = dot(turn, u4[...].reshape(256, D)).astype(BF).reshape(4, 4, 16, D)

    pass_cotangent()
    each(1, 16, lambda n: arrive(r1.at[0, lax.rem(me_zc + n, 16)], a_r.at[0, lax.rem(me_zc + n, 16)]))
    own_rows.wait()
    s2[0] = dot(turn, r1[0].reshape(256, D)).astype(BF).reshape(4, 4, 16, D)
    send_groups(0)
    take_weights(x_left, 0)
    weight_copy(4).start()
    take_weights(x_right, 1)
    weight_copy(5).start()
    grouped(0)
    take_weights(x_left, 1)
    take_weights(x_right, 0)

    tokens = r2[0].reshape(256, D).astype(F32)
    centre = jnp.mean(tokens, axis=-1, keepdims=True)
    shifted = tokens - centre
    inverse = lax.rsqrt(jnp.mean(shifted * shifted, axis=-1, keepdims=True) + EPS)
    standard = shifted * inverse
    std[...] = standard
    inv[...] = jnp.broadcast_to(inverse, (256, 128))
    gains = gain[...].reshape(1, D)
    normed = (standard * gains).astype(BF)
    nrm[...] = normed
    nt[...] = dot_nt(order, normed).astype(BF)
    ncot[...] = jnp.zeros((256, D), F32)
    br[...] = jnp.zeros((256, D), F32)

    lane = iota((64, 192), 1)
    head_mask = [(lane >= 64 * h) & (lane < 64 * h + 64) for h in range(3)]
    head_ones = [jnp.where(hm, 1.0, 0.0).astype(BF) for hm in head_mask]

    def stack_heads(rows):
        return jnp.concatenate([rows * ones for ones in head_ones], axis=0)

    def pick_heads(rows):
        return jnp.where(head_mask[0], rows[0:64], jnp.where(head_mask[1], rows[64:128], rows[128:192]))

    spots = [slice(64 * i, 64 * i + 64) for i in range(4)]

    def forward_step(j):
        for n in range(3):
            qkv[j, n] = dot_nt(nrm[...], wb[j, 192 * n : 192 * n + 192, :]).astype(BF)
        keep = [kept[spot, 0:1] > 0 for spot in spots]
        scores = [dot_nt(qkv[j, 1, spot], stack_heads(qkv[j, 0, spot])) for spot in spots]
        rounded = []
        for i in range(4):
            masked = jnp.where(keep[i], scores[i] * 0.125, -1000000000.0)
            expo = jnp.exp(masked - jnp.max(masked, axis=0, keepdims=True))
            weight = expo / jnp.sum(expo, axis=0, keepdims=True)
            wts[j, i] = weight
            rounded.append(weight.astype(BF))
        crossed = [dot_tn(rounded[i], qkv[j, 2, spot]) for i, spot in enumerate(spots)]
        mixed = [jnp.where(keep[i], pick_heads(crossed[i]), 0.0) for i in range(4)]
        mx[j] = jnp.concatenate(mixed, axis=0).astype(BF)
        br[...] += dot(mx[j], wb[j, 576:768, :])

    forward_step(x)

    def forward_rest(n, carry):
        j = lax.rem(x + 2 * n + 1 - 3 * (n // 2), 4)

        @pl.when(n == 1)
        def _():
            take_weights(x_far, 0)
            take_weights(x_far, 1)

        arrive(part(j, 1 - c, 0), f_r.at[j, 0])
        arrive(part(j, 1 - c, 1), f_r.at[j, 1])
        forward_step(j)
        return carry

    lax.fori_loop(0, 3, forward_rest, 0)

    def pack_result(k, block):
        for xx in range(4):
            cols = slice(192 * xx, 192 * xx + 192)
            for i2 in range(2):
                rb[k, xx, i2] = jnp.concatenate(
                    [block[128 * i2 : 128 * i2 + 64, cols], block[128 * i2 + 64 : 128 * i2 + 128, cols]], axis=1
                ).reshape(4, 16, 384)

    def result_copy(k, n):
        yy, xx, dev = yx_peer(n)
        return remote(rb.at[k, xx, :, yy], t1.at[k, x, y], p_s.at[k, xx, yy], p_r.at[k, x, y], dev)

    def own_result(k):
        return pltpu.make_async_copy(rb.at[k, x, :, y], t1.at[k, x, y], l_s.at[6 + k])

    def send_result(k):
        each(1, 16, lambda n: result_copy(k, n).start())
        own_result(k).start()

    def place_copy(k, g, n):
        s, dev = zc_peer(n)
        return remote(t2.at[k, g, s], ot.at[k, me_zc, g], q_s.at[k, g, s], q_r.at[k, g, me_zc], dev)

    def own_place(k, g):
        return pltpu.make_async_copy(t2.at[k, g, me_zc], ot.at[k, me_zc, g], l_s.at[10 + 2 * k + g])

    def relay(k):
        def got(n):
            yy, xx, _ = yx_peer(n)
            arrive(t1.at[k, xx, yy], p_r.at[k, xx, yy])

        each(1, 16, got)
        own_result(k).wait()
        for g in range(2):
            t2[k, g] = dot(turn, t1[k, 2 * g : 2 * g + 2].reshape(256, 384)).astype(BF).reshape(16, 16, 384)
            each(1, 16, lambda n: place_copy(k, g, n).start())
            own_place(k, g).start()

    def placed(k):
        for g in range(2):
            own_place(k, g).wait()
            each(1, 16, lambda n: arrive(ot.at[k, lax.rem(me_zc + n, 16), g], q_r.at[k, g, lax.rem(me_zc + n, 16)]))

    pack_result(0, (r2[0].reshape(256, D).astype(F32) + br[...]).astype(BF))
    send_result(0)

    take_cotangent()
    ctt[...] = dot_nt(order, r2[1].reshape(256, D)).astype(BF)

    def core_copy(jj):
        return remote(gb.at[jj, 1 - c], gc.at[jj], c_s.at[jj], c_r.at[jj], core_peer)

    def finish_core(jj):
        arrive(gc.at[jj], c_r.at[jj])
        hb[jj] = (gb[jj, c].astype(F32) + gc[jj].astype(F32)).astype(BF)

    left_cols, right_cols = pl.ds(0, 384), pl.ds(384, 384)

    def target(jj):
        return lax.rem(x + jj + 1, 4)

    def share_x(jj):
        return remote(hb.at[jj, :, left_cols], gx.at[x], x_s.at[jj], x_r.at[x], (m, target(jj)))

    def share_y(jj, n):
        yy, dev = y_peer(n)
        return remote(
            hb.at[jj, pl.ds(yy * 96, 96), right_cols], gy1.at[jj, y], y1_s.at[jj, yy], y1_r.at[jj, y], dev
        )

    def start_shares(jj):
        for n in (1, 3, 2):
            share_y(jj, n).start()

    def backward_step(jj, carry):
        j = target(jj)
        mc = dot_nt(r2[1].reshape(256, D), wb[j, 576:768, :])
        mcs[...] = jnp.where(kept[:, 0:1] > 0, mc, 0.0).astype(BF)
        mcb = [stack_heads(mcs[spot]) for spot in spots]
        dws = [dot_nt(qkv[j, 2, spot], mcb[i]) for i, spot in enumerate(spots)]
        dv = [dot(wts[j, i].astype(BF), mcb[i]) for i in range(4)]
        dscores = []
        for i in range(4):
            weight = wts[j, i]
            inner = jnp.sum(dws[i] * weight, axis=0, keepdims=True)
            dscores.append((weight * (dws[i] - inner) * 0.125).astype(BF))
        dk = [dot(dscores[i], stack_heads(qkv[j, 0, spot])) for i, spot in enumerate(spots)]
        dq = [pick_heads(dot_tn(dscores[i], qkv[j, 1, spot])) for i, spot in enumerate(spots)]
        for n, pieces in enumerate((dq, dk, dv)):
            dp[n] = jnp.concatenate(pieces, axis=0).astype(BF)
        for n in range(3):
            pcm[:, 192 * n : 192 * n + 192] = dp[n]
        pcm[:, 576:768] = mx[j]
        low = iota((256, 256), 1) < 64
        tail = pcm[:, 512:768]
        tail_qkv = jnp.where(low, tail, jnp.zeros_like(tail))
        tail_mix = jnp.where(low, jnp.zeros_like(tail), tail)
        for h in range(2):
            rows = slice(384 * h, 384 * h + 384)
            gb[jj, h, :, 0:512] = dot(nt[rows, :], pcm[:, 0:512]).astype(BF)
            gb[jj, h, :, 512:768] = (dot(nt[rows, :], tail_qkv) + dot(ctt[rows, :], tail_mix)).astype(BF)
        core_copy(jj).start()
        ncot[...] += (
            dot(dp[0], wb[j, 0:192, :]) + dot(dp[1], wb[j, 192:384, :]) + dot(dp[2], wb[j, 384:576, :])
        )

        @pl.when(jj > 0)
        def _():
            finish_core(jj - 1)

        @pl.when((jj > 0) & (jj < EARLY + 1))
        def _():
            share_x(jj - 1).start()
            start_shares(jj - 1)

        @pl.when(jj == RELAY)
        def _():
            relay(0)

        return carry

    lax.fori_loop(0, 4, backward_step, 0)

    cotangent = ncot[...].astype(BF).astype(F32)
    standard = std[...]
    scaled = cotangent * gains
    mean_plain = jnp.mean(scaled, axis=-1, keepdims=True)
    mean_cross = jnp.mean(scaled * standard, axis=-1, keepdims=True)
    through = inv[:, 0:1] * (scaled - mean_plain - standard * mean_cross)
    pack_result(1, (r2[1].reshape(256, D).astype(F32) + through).astype(BF))
    send_result(1)
    for jj in range(EARLY, 3):
        share_x(jj).start()
        start_shares(jj)

    gain_part = jnp.sum(cotangent * standard, axis=0, keepdims=True)
    vg[0] = jnp.concatenate(
        [gain_part[:, 192 * k : 192 * k + 192] for k in range(4)] + [jnp.zeros((4, 192), F32)], axis=0
    )
    gain_core = remote(vg.at[0], vgc, vc_s, vc_r, core_peer)
    gain_core.start()
    finish_core(3)
    start_shares(3)

    def share_x2(jj):
        return remote(hy1.at[jj], gx2.at[x], x2_s.at[jj], x2_r.at[x], (m, target(jj)))

    def sum_y1(jj):
        total = hb[jj, pl.ds(pl.multiple_of(y * 96, 16), 96), 384:768].astype(F32)
        for n in range(1, 4):
            yy = lax.rem(y + n, 4)
            arrive(gy1.at[jj, yy], y1_r.at[jj, yy])
            total = total + gy1[jj, yy].astype(F32)
        hy1[jj] = total.astype(BF)

    def sum_y1_send(jj):
        sum_y1(jj)
        share_x2(jj).start()

    relay(1)
    each(0, 3, sum_y1_send)

    total = hb[3, :, 0:384].astype(F32)
    for n in range(1, 4):
        xx = lax.rem(x + n, 4)
        arrive(gx.at[xx], x_r.at[xx])
        total = total + gx[xx].astype(F32)
    hx[...] = total.astype(BF).reshape(4, 96, 384)

    def share_y2(n):
        yy, dev = y_peer(n)
        return remote(hx.at[yy], gy2.at[y], y2_s.at[yy], y2_r.at[y], dev)

    for n in (1, 3, 2):
        share_y2(n).start()

    arrive(vgc, vc_r)
    vg[1] = vg[0] + vgc[...]

    def gain_x(n):
        xx, dev = x_peer(n)
        return remote(vg.at[1], vgx.at[x], vx_s.at[xx], vx_r.at[x], dev)

    for n in range(1, 4):
        gain_x(n).start()

    sum_y1(3)

    gain_total = vg[1]
    for n in range(1, 4):
        xx = lax.rem(x + n, 4)
        arrive(vgx.at[xx], vx_r.at[xx])
        gain_total = gain_total + vgx[xx]
    vg[2] = gain_total

    def gain_y(n):
        yy, dev = y_peer(n)
        return remote(vg.at[2], vgy.at[y], vy_s.at[yy], vy_r.at[y], dev)

    for n in range(1, 4):
        gain_y(n).start()

    left = hx[y].astype(F32)
    right = hy1[3].astype(F32)
    for n in range(1, 4):
        yy = lax.rem(y + n, 4)
        xx = lax.rem(x + n, 4)
        arrive(gy2.at[yy], y2_r.at[yy])
        arrive(gx2.at[xx], x2_r.at[xx])
        left = left + gy2[yy].astype(F32)
        right = right + gx2[xx].astype(F32)
    spread = spread_matrix()
    gzs[:, :, 0:384] = dot(spread, left.astype(BF)).astype(BF).reshape(8, 16, 384)
    gzs[:, :, 384:768] = dot(spread, right.astype(BF)).astype(BF).reshape(8, 16, 384)

    def grad_z(n):
        zz, dev = z_peer(n)
        return remote(gzs.at[zz], gz.at[z], z_s.at[zz], z_r.at[z], dev)

    for n in range(1, 8):
        grad_z(n).start()

    gain_total = vg[2]
    for n in range(1, 4):
        yy = lax.rem(y + n, 4)
        arrive(vgy.at[yy], vy_r.at[yy])
        gain_total = gain_total + vgy[yy]
    vg[3] = gain_total

    def gain_z(n):
        zz, dev = z_peer(n)
        return remote(vg.at[3], vgz.at[z], vz_s.at[zz], vz_r.at[z], dev)

    for n in range(1, 8):
        gain_z(n).start()


    total = gzs[z].astype(F32)
    gain_total = vg[3]
    for n in range(1, 8):
        zz = lax.rem(z + n, 8)
        arrive(gz.at[zz], z_r.at[zz])
        arrive(vgz.at[zz], vz_r.at[zz])
        total = total + gz[zz].astype(F32)
        gain_total = gain_total + vgz[zz]
    o_gr[...] = total
    o_gg[...] = jnp.broadcast_to(
        jnp.sum(jnp.where(iota((8, 192), 0) == x, gain_total, 0.0), axis=0, keepdims=True), (8, 192)
    )

    placed(0)
    placed(1)

    def sent(n):
        for k in range(2):
            token_copy(k, n).wait_send()
            result_copy(k, n).wait_send()
            for g in range(2):
                place_copy(k, g, n).wait_send()

    each(1, 16, sent)
    for n in range(6):
        weight_copy(n).wait_send()
    for n in range(1, 4):
        xx = lax.rem(x + n, 4)
        swap_copy(xx, 0).wait_send()
        swap_copy(xx, 1).wait_send()
        group_copy(0, n).wait_send()
        group_copy(1, n).wait_send()
        gain_x(n).wait_send()
        share_y2(n).wait_send()
        gain_y(n).wait_send()

        def sent_y(jj):
            share_y(jj, n).wait_send()

        each(0, 4, sent_y)
    each(0, 4, lambda jj: core_copy(jj).wait_send())
    each(0, 3, lambda jj: share_x(jj).wait_send())
    each(0, 3, lambda jj: share_x2(jj).wait_send())
    for n in range(1, 8):
        grad_z(n).wait_send()
        gain_z(n).wait_send()
    gain_core.wait_send()


def finish(ot, gr, gg, o_bo, o_gi, o_gq, o_gp, o_gg):
    unpair = unpair_matrix()
    for k, out in enumerate((o_bo, o_gi)):
        for b in range(4):
            rows = ot[k, 4 * b : 4 * b + 4].reshape(128, 384)
            both = jnp.concatenate([rows[:, 0:192], rows[:, 192:384]], axis=0)
            out[:, 256 * b : 256 * b + 256] = dot_tn(both, unpair).astype(BF)
    total = gr[0:12, :]
    for n in range(3):
        o_gq[:, n, :] = total[:, 192 * n : 192 * n + 192].astype(BF)
    o_gp[...] = total[:, 576:768].astype(BF)
    o_gg[...] = gg[0, :]


def body(frames_in, norm_gain, w_qkv, w_out, keep_runs, out_cotangent):
    v = lambda shape, dt=BF: pltpu.VMEM(shape, dt)
    dma = pltpu.SemaphoreType.DMA
    any_spec = pl.BlockSpec(memory_space=pl.ANY)
    vmem_spec = pl.BlockSpec(memory_space=pltpu.VMEM)
    placed, grads, gain_sum = pl.pallas_call(
        kernel,
        out_shape=(
            jax.ShapeDtypeStruct((2, 16, 2, 16, 384), BF),
            jax.ShapeDtypeStruct((16, D), F32),
            jax.ShapeDtypeStruct((8, 192), F32),
        ),
        in_specs=[any_spec, any_spec, vmem_spec, any_spec, any_spec, vmem_spec],
        out_specs=(any_spec, vmem_spec, vmem_spec),
        scratch_shapes=[
            v((2, 16, 16, D)),
            v((2, 4, 4, 16, D)),
            v((4, 4, 16, D)),
            v((16, 16, D)),
            v((16, 16, D)),
            v((2, 4, 4, 16, D)),
            v((4, D, D)),
            v((256, D), F32),
            v((256, 128), F32),
            v((256, D)),
            v((D, 256)),
            v((D, 256)),
            v((256, D), F32),
            v((256, D), F32),
            v((256, 128), F32),
            v((4, 3, 256, 192)),
            v((4, 4, 64, 192), F32),
            v((4, 256, 192)),
            v((256, 192)),
            v((3, 256, 192)),
            v((256, D)),
            v((4, 2, 384, D)),
            v((4, 384, D)),
            v((4, 384, D)),
            v((4, 384, 384)),
            v((4, 4, 96, 384)),
            v((4, 96, 384)),
            v((4, 96, 384)),
            v((4, 96, 384)),
            v((4, 96, 384)),
            v((8, 16, D)),
            v((8, 16, D)),
            v((2, 4, 2, 4, 16, 384)),
            v((2, 4, 4, 2, 16, 384)),
            v((2, 2, 16, 16, 384)),
            v((4, 8, 192), F32),
            v((8, 192), F32),
            v((4, 8, 192), F32),
            v((4, 8, 192), F32),
            v((8, 8, 192), F32),
            dma((2, 16)), dma((2, 16)),
            dma((2, 4)), dma((2, 4)),
            dma((6,)), dma((4, 2)),
            dma((4, 2)), dma((4, 2)),
            dma((4,)), dma((4,)),
            dma((4,)), dma((4,)),
            dma((4, 4)), dma((4, 4)),
            dma((4,)), dma((4,)),
            dma((4,)), dma((4,)),
            dma((8,)), dma((8,)),
            dma((2, 4, 4)), dma((2, 4, 4)),
            dma((2, 2, 16)), dma((2, 2, 16)),
            dma(()), dma(()),
            dma((4,)), dma((4,)),
            dma((4,)), dma((4,)),
            dma((8,)), dma((8,)),
            dma((15,)),
        ],
        compiler_params=pltpu.CompilerParams(
            collective_id=0, has_side_effects=True, vmem_limit_bytes=56 << 20
        ),
        cost_estimate=pl.CostEstimate(flops=5 * 10**9, bytes_accessed=10**7, transcendentals=200000),
        name="block",
    )(
        frames_in.reshape(1024, D),
        out_cotangent.reshape(16, 4, 16, D),
        norm_gain,
        w_qkv.transpose(1, 2, 0).reshape(576, D),
        w_out,
        keep_runs.transpose(1, 2, 0),
    )
    block_out, grad_in, grad_qkv, grad_proj, grad_gain = pl.pallas_call(
        finish,
        out_shape=(
            jax.ShapeDtypeStruct((192, 1024), BF),
            jax.ShapeDtypeStruct((192, 1024), BF),
            jax.ShapeDtypeStruct((12, 3, 192), BF),
            jax.ShapeDtypeStruct((12, 192), BF),
            jax.ShapeDtypeStruct((192,), F32),
        ),
        in_specs=[vmem_spec] * 3,
        out_specs=(vmem_spec,) * 5,
        compiler_params=pltpu.CompilerParams(vmem_limit_bytes=60 << 20),
        cost_estimate=pl.CostEstimate(flops=4 * 10**8, bytes_accessed=3 * 10**6, transcendentals=0),
        name="finish",
    )(placed, grads, gain_sum)
    return (
        block_out.T.reshape(1, 1024, 192),
        grad_in.T.reshape(1, 1024, 192),
        grad_qkv,
        grad_proj.T,
        grad_gain,
    )


def solution(mesh):
    in_specs = (
        P("tm", None, None),
        P(),
        P(None, None, "tensor"),
        P("tensor", None),
        P(),
        P("tm", None, None),
    )
    out_specs = (
        P("tm", None, "tensor"),
        P("tm", None, "tensor"),
        P("tm", None, "tensor"),
        P("tensor", "tm"),
        P("tensor"),
    )
    return jax.shard_map(body, mesh=mesh, in_specs=in_specs, out_specs=out_specs, check_vma=False)
```
